128 devices in a mesh: frames: 32 (over z, y, x_hi), rows: 4 (over x_lo, core).
Axes of the slice: x: 4 (x_hi: 2, x_lo: 2; x = x_hi * 2 + x_lo), y: 4, z: 4, core: 2. Of those that a mesh axis runs over, the one named last changes fastest.
Arguments:
- inputs: bfloat16 [256, 16, 64, 256], P('frames', 'rows'), may hold values from -40 to 40
- kernel_one: bfloat16 [3, 3, 3, 256, 256], replicated, may hold values from -0.078125 to 0.078125
- gain_one: float32 [256], replicated, may hold values from 0.1 to 1.9
- offset_one: float32 [256], replicated, may hold values from -3 to 3
- kernel_two: bfloat16 [3, 3, 3, 256, 256], replicated, may hold values from -0.078125 to 0.078125
- gain_two: float32 [256], replicated, may hold values from 0.1 to 1.9
- offset_two: float32 [256], replicated, may hold values from -3 to 3
- bias_two: float32 [256], replicated, may hold values from -3 to 3
Outputs:
- low_band: bfloat16 [128, 8, 32, 256], P('frames', None, 'rows')
- high_bands: bfloat16 [7, 128, 8, 32, 256], P(None, 'frames', 'rows')
The draws below stay inside these ranges and needn't reach their ends.
All inputs are finite; a program needn't handle non-finite values.
Results may differ from the reference program's by a relative error of at most 0.009.
Values may be sent and summed in bfloat16 or wider, within the bound.
No kernel may reach another device: no remote copies, remote signals or barrier semaphores. Data moves between devices by JAX's collectives and lax.ppermute only.
A program may use at most 192 MiB of HBM per device.

```python
import math
import jax
import jax.numpy as jnp
from jax import lax

CHANNELS = 256
GROUPS = 32
WIDTH = 64
FRAMES = 256
HEIGHT = 16


def draw_inputs(key, part):
    key = jax.random.fold_in(key, 7)
    keys = jax.random.split(key, 5)
    shape = (FRAMES, HEIGHT, WIDTH, CHANNELS)
    base = jax.random.normal(keys[0], shape, jnp.float32)
    ramp_base = 3.0
    position = jnp.arange(FRAMES, dtype=jnp.float32) / max(FRAMES - 1, 1)
    frame_scale = ramp_base ** position * jnp.exp(jax.random.uniform(keys[1], (FRAMES,), jnp.float32, math.log(0.5), math.log(2.0)))
    row_scale = jnp.exp(jax.random.uniform(keys[2], (HEIGHT,), jnp.float32, math.log(0.6), math.log(1.6)))
    column_scale = jnp.exp(jax.random.uniform(keys[3], (WIDTH,), jnp.float32, math.log(0.7), math.log(1.4)))
    channel_scale = jnp.exp(jax.random.uniform(keys[4], (CHANNELS,), jnp.float32, math.log(0.5), math.log(2.0)))
    values = base * frame_scale[:, None, None, None] * row_scale[None, :, None, None]
    values = values * column_scale[None, None, :, None] * channel_scale
    return jnp.clip(values / 1.8, -40.0, 40.0).astype(jnp.bfloat16)


def noise(stream_key, extent, scale, reach, held_as=jnp.bfloat16):
    array = scale * jax.random.normal(stream_key, extent, jnp.float32)
    return jnp.clip(array, min=-reach, max=reach).astype(held_as)


def setup_inputs(seed: int = 0) -> dict:
    streams_of = jax.random.split(jax.random.key(seed), 9)
    inputs = draw_inputs(jax.random.fold_in(streams_of[8], 71), 0)
    kernel_one = noise(streams_of[1], (3, 3, 3, CHANNELS, CHANNELS), (27 * CHANNELS) ** -0.5, 0.078125)
    gain_one = jnp.clip(1.0 + 0.18 * jax.random.normal(streams_of[2], (CHANNELS,), jnp.float32), 0.1, 1.9)
    offset_one = noise(streams_of[3], (CHANNELS,), 0.5, 3.0, jnp.float32)
    kernel_two = noise(streams_of[4], (3, 3, 3, CHANNELS, CHANNELS), (27 * CHANNELS) ** -0.5, 0.078125)
    gain_two = jnp.clip(1.0 + 0.18 * jax.random.normal(streams_of[5], (CHANNELS,), jnp.float32), 0.1, 1.9)
    offset_two = noise(streams_of[6], (CHANNELS,), 0.5, 3.0, jnp.float32)
    bias_two = noise(streams_of[7], (CHANNELS,), 0.5, 3.0, jnp.float32)
    return {"inputs": inputs, "kernel_one": kernel_one, "gain_one": gain_one, "offset_one": offset_one, "kernel_two": kernel_two, "gain_two": gain_two, "offset_two": offset_two, "bias_two": bias_two}


EPS = 1e-06

def group_norm(values, gain, offset):
    shape = values.shape
    grouped = values.reshape(shape[:-1] + (GROUPS, shape[-1] // GROUPS))
    mean = lax.optimization_barrier(jnp.mean(grouped, axis=(0, 1, 2, 4), keepdims=True))
    centred = grouped - mean
    var = lax.optimization_barrier(jnp.mean(centred * centred, axis=(0, 1, 2, 4), keepdims=True))
    normed = (centred / jnp.sqrt(var + EPS)).reshape(shape)
    return normed * gain + offset

def conv_causal(active, kernel):
    frames_all, height, width, chans = active.shape
    padded = jnp.pad(active.astype(jnp.float32), ((2, 0), (1, 1), (1, 1), (0, 0)))
    weights = kernel.astype(jnp.float32)

    def one_frame(index):
        window = lax.dynamic_slice_in_dim(padded, index, 3, 0)
        total = jnp.zeros((height * width, weights.shape[-1]), jnp.float32)
        for lag_time in range(3):
            for lag_row in range(3):
                for lag_col in range(3):
                    piece = window[lag_time, lag_row:lag_row + height, lag_col:lag_col + width].reshape(-1, chans)
                    total = total + jnp.dot(piece, weights[lag_time, lag_row, lag_col], precision=lax.Precision.HIGHEST, preferred_element_type=jnp.float32)
        return total.reshape(height, width, -1)
    return lax.map(one_frame, jnp.arange(frames_all, dtype=jnp.int32))

def haar_split(field):
    frames_all, height, width, chans = field.shape
    blocks = field.reshape(frames_all // 2, 2, height // 2, 2, width // 2, 2, chans)
    factor = 1.0 / jnp.sqrt(jnp.float32(2.0))
    pieces = [blocks]
    for axis in (1, 2, 3):
        following = []
        for piece in pieces:
            first = jnp.take(piece, 0, axis=axis)
            second = jnp.take(piece, 1, axis=axis)
            following.append((first + second) * factor)
            following.append((first - second) * factor)
        pieces = following
    return (pieces[0], jnp.stack(pieces[1:], 0))

def reference(inputs, kernel_one, gain_one, offset_one, kernel_two, gain_two, offset_two, bias_two):
    source = inputs.astype(jnp.float32)
    act_one = jax.nn.silu(group_norm(source, gain_one, offset_one)).astype(jnp.bfloat16)
    hidden = conv_causal(act_one, kernel_one).astype(jnp.bfloat16)
    act_two = jax.nn.silu(group_norm(hidden.astype(jnp.float32), gain_two, offset_two)).astype(jnp.bfloat16)
    summed = source + conv_causal(act_two, kernel_two) + bias_two
    low, high = haar_split(summed)
    return (low.astype(jnp.bfloat16), high.astype(jnp.bfloat16))
```

```python
import functools

import jax
import jax.numpy as jnp
from jax import lax
from jax.experimental import pallas as pl
from jax.experimental.pallas import tpu as pltpu
from jax.sharding import PartitionSpec as P

GROUPS = 32
EPS = 1e-06
VMEM = pl.BlockSpec(memory_space=pltpu.VMEM)
LANES = 128
HIGHEST = lax.Precision.HIGHEST


def exact_dot(left, right):
    return jnp.dot(left, right, precision=HIGHEST, preferred_element_type=jnp.float32)


def group_of_channel(rows, cols, row_is_channel, span, shift):
    row = lax.broadcasted_iota(jnp.int32, (rows, cols), 0)
    col = lax.broadcasted_iota(jnp.int32, (rows, cols), 1)
    channel, lane = (row, col) if row_is_channel else (col, row)
    return jnp.where(channel // span + shift == lane, 1.0, 0.0)


def local_stats(values_ref, out_ref):
    frames, rows, cols, chans = values_ref.shape
    span = chans // GROUPS
    count = float(frames * rows * cols * span)

    def block(index):
        return values_ref[index].astype(jnp.float32).reshape(rows * cols // 8, 8, chans)

    def add_sum(index, total):
        return total + jnp.sum(block(index), axis=0)

    total = lax.fori_loop(0, frames, add_sum, jnp.zeros((8, chans), jnp.float32))
    gather = group_of_channel(chans, LANES, True, span, 0)
    spread = group_of_channel(LANES, chans, False, span, 0)
    means = jnp.sum(exact_dot(total, gather), axis=0, keepdims=True) / count
    means = jnp.broadcast_to(means, (8, LANES))
    centre = exact_dot(means, spread)

    def add_square(index, total):
        away = block(index) - centre
        return total + jnp.sum(away * away, axis=0)

    squares = lax.fori_loop(0, frames, add_square, jnp.zeros((8, chans), jnp.float32))
    gather_high = group_of_channel(chans, LANES, True, span, GROUPS)
    squares = jnp.sum(exact_dot(squares, gather_high), axis=0, keepdims=True)
    out_ref[...] = jnp.broadcast_to(means[0:1] + squares, out_ref.shape)


def norm_terms(stats_ref, gain_ref, chans, count):
    stats = stats_ref[...]
    devices = stats.shape[0]
    average = jnp.sum(stats, axis=0, keepdims=True) / devices
    away = stats - average
    between = jnp.sum(away * away, axis=0, keepdims=True) / devices
    lane = lax.broadcasted_iota(jnp.int32, (1, LANES), 1)
    first = jnp.where(lane < GROUPS, average, 0.0)
    second = jnp.where(lane < GROUPS, between, jnp.where(lane < 2 * GROUPS, average / count, 0.0))
    span = chans // GROUPS
    spread = group_of_channel(LANES, chans, False, span, 0) + group_of_channel(
        LANES, chans, False, span, GROUPS
    )
    mean = exact_dot(jnp.broadcast_to(first, (8, LANES)), spread)[0:1]
    var = exact_dot(jnp.broadcast_to(second, (8, LANES)), spread)[0:1]
    return mean, gain_ref[...] / jnp.sqrt(var + EPS)


def build_windows(
    own_ref, past_ref, near_ref, far_ref, near_past_ref, far_past_ref, mean, scale, offset, wide_ref
):
    frames, rows, cols, chans = own_ref.shape
    frame_place = lax.axis_index("frames")
    row_place = lax.axis_index("rows")
    odd = lax.rem(row_place, 2) == 1
    has_past = frame_place > 0
    has_above = row_place > 0
    has_below = row_place < lax.axis_size("rows") - 1
    column = lax.broadcasted_iota(jnp.int32, (cols, chans), 0)

    def put(frame, row, value, valid):
        value = (value.astype(jnp.float32) - mean) * scale + offset
        value = 0.5 * value * (1.0 + jnp.tanh(0.5 * value))
        if valid is not None:
            value = jnp.where(valid, value, 0.0)
        left = jnp.where(column == 0, 0.0, pltpu.roll(value, 1, 0))
        right = jnp.where(column == cols - 1, 0.0, pltpu.roll(value, cols - 1, 0))
        wide_ref[frame, row, :, 0:chans] = left.astype(jnp.bfloat16)
        wide_ref[frame, row, :, chans : 2 * chans] = value.astype(jnp.bfloat16)
        wide_ref[frame, row, :, 2 * chans :] = right.astype(jnp.bfloat16)

    def edges(frame, near, far, valid):
        above = jnp.logical_and(has_above, valid)
        below = jnp.logical_and(has_below, valid)
        put(frame, 0, jnp.where(odd, near, far), above)
        put(frame, rows + 1, jnp.where(odd, far, near), below)

    def past(frame, carry):
        for row in range(rows):
            put(frame, row + 1, past_ref[frame, row], has_past)
        edges(frame, near_past_ref[frame], far_past_ref[frame], has_past)
        return carry

    def own(frame, carry):
        for row in range(rows):
            put(frame + 2, row + 1, own_ref[frame, row], None)
        edges(frame + 2, near_ref[frame], far_ref[frame], True)
        return carry

    lax.fori_loop(0, 2, past, 0)
    lax.fori_loop(0, frames, own, 0)


def conv_frames(wide_ref, kernel_ref, start, count, rows, cols, chans):
    total = None
    for lag_time in range(3):
        for lag_row in range(3):
            window = wide_ref[pl.ds(start + lag_time, count), lag_row : lag_row + rows]
            term = jnp.dot(
                window.reshape(count * rows * cols, 3 * chans),
                kernel_ref[lag_time, lag_row],
                preferred_element_type=jnp.float32,
            )
            total = term if total is None else total + term
    return total.reshape(count, rows, cols, -1)


def columns_apart(line, pair_ref):
    cols, chans = line.shape
    halves = range(chans // LANES)
    for half in halves:
        pair_ref[half] = line[:, half * LANES : (half + 1) * LANES]
    return (
        jnp.concatenate([pair_ref[half, pl.ds(k, cols // 2, stride=2)] for half in halves], axis=1)
        for k in range(2)
    )


def stats_kernel(values_ref, out_ref):
    local_stats(values_ref, out_ref)


def first_kernel(
    own_ref, past_ref, near_ref, far_ref, near_past_ref, far_past_ref,
    stats_ref, gain_ref, offset_ref, kernel_ref,
    hidden_ref, out_stats_ref, wide_ref,
):
    frames, rows, cols, chans = own_ref.shape
    count = frames * rows * cols * (chans // GROUPS)
    mean, scale = norm_terms(stats_ref, gain_ref, chans, count)
    build_windows(
        own_ref, past_ref, near_ref, far_ref, near_past_ref, far_past_ref,
        mean, scale, offset_ref[...], wide_ref,
    )
    step = 2

    def some(index, carry):
        start = index * step
        conv = conv_frames(wide_ref, kernel_ref, start, step, rows, cols, chans)
        hidden_ref[pl.ds(start, step)] = conv.astype(jnp.bfloat16)
        return carry

    lax.fori_loop(0, frames // step, some, 0)
    local_stats(hidden_ref, out_stats_ref)


def second_kernel(
    own_ref, past_ref, near_ref, far_ref, near_past_ref, far_past_ref,
    stats_ref, gain_ref, offset_ref, kernel_ref, source_ref, bias_ref,
    low_ref, high_ref, wide_ref, pair_ref,
):
    frames, rows, cols, chans = own_ref.shape
    count = frames * rows * cols * (chans // GROUPS)
    mean, scale = norm_terms(stats_ref, gain_ref, chans, count)
    build_windows(
        own_ref, past_ref, near_ref, far_ref, near_past_ref, far_past_ref,
        mean, scale, offset_ref[...], wide_ref,
    )
    factor = 0.5 ** 1.5
    bands = low_ref.shape[0]
    width = cols // 2 // bands

    def some(index, carry):
        start = index * 2
        conv = conv_frames(wide_ref, kernel_ref, start, 2, rows, cols, chans)
        summed = source_ref[pl.ds(start, 2)].astype(jnp.float32) + conv + bias_ref[...]
        for time_band in range(2):
            mixed = summed[0] - summed[1] if time_band else summed[0] + summed[1]
            for pair in range(rows // 2):
                upper, lower = mixed[2 * pair], mixed[2 * pair + 1]
                for row_band in range(2):
                    line = (upper - lower if row_band else upper + lower) * factor
                    even, uneven = columns_apart(line, pair_ref)
                    for col_band in range(2):
                        value = even - uneven if col_band else even + uneven
                        value = value.astype(jnp.bfloat16)
                        band = 4 * time_band + 2 * row_band + col_band
                        if band:
                            high_ref[band - 1, index, pair] = value
                        else:
                            for target in range(bands):
                                low_ref[target, index, pair] = value[
                                    target * width : (target + 1) * width
                                ]
        return carry

    lax.fori_loop(0, frames // 2, some, 0)


def exchange(values):
    frame_count, row_count = lax.axis_size("frames"), lax.axis_size("rows")
    axes = ("frames", "rows")
    odd = lax.rem(lax.axis_index("rows"), 2) == 1
    rows = values.shape[1]
    top, bottom = values[:, 0], values[:, rows - 1]
    near = jnp.where(odd, top, bottom)
    far = jnp.where(odd, bottom, top)

    def place(frame, row):
        return frame * row_count + row

    every = range(frame_count)
    later = range(frame_count - 1)
    near_rows = [(r, r ^ 1) for r in range(row_count) if (r ^ 1) < row_count]
    far_rows = [(r, ((r + 1) ^ 1) - 1) for r in range(1, row_count - 1)]

    def route(frames, shift, pairs):
        return [(place(f, r), place(f + shift, s)) for f in frames for r, s in pairs]

    same = [(r, r) for r in range(row_count)]
    past = lax.ppermute(values[-2:], axes, route(later, 1, same))
    got_near = lax.ppermute(near, axes, route(every, 0, near_rows))
    got_far = lax.ppermute(far, axes, route(every, 0, far_rows))
    got_near_past = lax.ppermute(near[-2:], axes, route(later, 1, near_rows))
    got_far_past = lax.ppermute(far[-2:], axes, route(later, 1, far_rows))
    return past, got_near, got_far, got_near_past, got_far_past


def share(stats):
    return lax.all_to_all(stats, ("frames", "rows"), 0, 0, tiled=True)


def body(inputs, kernel_one, gain_one, offset_one, kernel_two, gain_two, offset_two, bias_two):
    frames, rows, cols, chans = inputs.shape
    devices = lax.axis_size("frames") * lax.axis_size("rows")
    bands = lax.axis_size("rows")
    stats_shape = jax.ShapeDtypeStruct((devices, LANES), jnp.float32)
    wide = pltpu.VMEM((frames + 2, rows + 2, cols, 3 * chans), jnp.bfloat16)
    weights_one = kernel_one.reshape(3, 3, 3 * chans, chans)
    weights_two = kernel_two.reshape(3, 3, 3 * chans, chans)

    stats_one = pl.pallas_call(
        stats_kernel, out_shape=stats_shape, in_specs=[VMEM], out_specs=VMEM,
        compiler_params=pltpu.CompilerParams(vmem_limit_bytes=8 * 2**20),
        name="stats_one",
    )(inputs)
    parts = exchange(inputs)
    stats_one = share(stats_one)
    hidden, stats_two = pl.pallas_call(
        first_kernel,
        out_shape=(jax.ShapeDtypeStruct(inputs.shape, jnp.bfloat16), stats_shape),
        in_specs=[VMEM] * 10, out_specs=(VMEM, VMEM), scratch_shapes=[wide],
        compiler_params=pltpu.CompilerParams(vmem_limit_bytes=32 * 2**20),
        name="conv_one",
    )(inputs, *parts, stats_one, gain_one[None], offset_one[None], weights_one)
    stats_two = share(stats_two)
    parts = exchange(hidden)
    low, high = pl.pallas_call(
        second_kernel,
        out_shape=(
            jax.ShapeDtypeStruct(
                (bands, frames // 2, rows // 2, cols // 2 // bands, chans), jnp.bfloat16
            ),
            jax.ShapeDtypeStruct((7, frames // 2, rows // 2, cols // 2, chans), jnp.bfloat16),
        ),
        in_specs=[VMEM] * 12, out_specs=(VMEM, VMEM),
        scratch_shapes=[wide, pltpu.VMEM((chans // LANES, cols, LANES), jnp.float32)],
        compiler_params=pltpu.CompilerParams(vmem_limit_bytes=32 * 2**20),
        name="conv_two",
    )(
        hidden, *parts, stats_two, gain_two[None], offset_two[None], weights_two, inputs,
        bias_two[None],
    )
    tiles = lax.all_to_all(low, "rows", split_axis=0, concat_axis=0, tiled=True)
    tiles = jnp.transpose(tiles, (1, 0, 2, 3, 4)).reshape(
        frames // 2, bands * (rows // 2), cols // 2 // bands, chans
    )
    return tiles, high


def solution(mesh):
    in_specs = (P("frames", "rows", None, None), P(), P(), P(), P(), P(), P(), P())
    out_specs = (P("frames", None, "rows", None), P(None, "frames", "rows", None, None))
    return jax.shard_map(body, mesh=mesh, in_specs=in_specs, out_specs=out_specs, check_vma=False)
```

```python
import functools

import jax
import jax.numpy as jnp
from jax import lax
from jax.experimental import pallas as pl
from jax.experimental.pallas import tpu as pltpu
from jax.sharding import PartitionSpec as P

GROUPS = 32
EPS = 1e-06
VMEM = pl.BlockSpec(memory_space=pltpu.VMEM)
LANES = 128
HIGHEST = lax.Precision.HIGHEST


def exact_dot(left, right):
    return jnp.dot(left, right, precision=HIGHEST, preferred_element_type=jnp.float32)


def group_of_channel(rows, cols, row_is_channel, span, shift):
    row = lax.broadcasted_iota(jnp.int32, (rows, cols), 0)
    col = lax.broadcasted_iota(jnp.int32, (rows, cols), 1)
    channel, lane = (row, col) if row_is_channel else (col, row)
    return jnp.where(channel // span + shift == lane, 1.0, 0.0)


def local_stats(values_ref, first, out_ref):
    last, rows, cols, chans = values_ref.shape
    frames = last - first
    span = chans // GROUPS
    count = float(frames * rows * cols * span)

    def block(index):
        return values_ref[index].astype(jnp.float32).reshape(rows * cols // 8, 8, chans)

    def add_sum(index, total):
        return total + jnp.sum(block(index), axis=0)

    total = lax.fori_loop(first, last, add_sum, jnp.zeros((8, chans), jnp.float32))
    gather = group_of_channel(chans, LANES, True, span, 0)
    spread = group_of_channel(LANES, chans, False, span, 0)
    means = jnp.sum(exact_dot(total, gather), axis=0, keepdims=True) / count
    means = jnp.broadcast_to(means, (8, LANES))
    centre = exact_dot(means, spread)

    def add_square(index, total):
        away = block(index) - centre
        return total + jnp.sum(away * away, axis=0)

    squares = lax.fori_loop(first, last, add_square, jnp.zeros((8, chans), jnp.float32))
    gather_high = group_of_channel(chans, LANES, True, span, GROUPS)
    squares = jnp.sum(exact_dot(squares, gather_high), axis=0, keepdims=True)
    out_ref[...] = jnp.broadcast_to(means[0:1] + squares, out_ref.shape)


def norm_terms(stats_ref, gain_ref, chans, count):
    stats = stats_ref[...]
    devices = stats.shape[0]
    average = jnp.sum(stats, axis=0, keepdims=True) / devices
    away = stats - average
    between = jnp.sum(away * away, axis=0, keepdims=True) / devices
    lane = lax.broadcasted_iota(jnp.int32, (1, LANES), 1)
    first = jnp.where(lane < GROUPS, average, 0.0)
    second = jnp.where(lane < GROUPS, between, jnp.where(lane < 2 * GROUPS, average / count, 0.0))
    span = chans // GROUPS
    spread = group_of_channel(LANES, chans, False, span, 0) + group_of_channel(
        LANES, chans, False, span, GROUPS
    )
    mean = exact_dot(jnp.broadcast_to(first, (8, LANES)), spread)[0:1]
    var = exact_dot(jnp.broadcast_to(second, (8, LANES)), spread)[0:1]
    return mean, gain_ref[...] / jnp.sqrt(var + EPS)


def near_and_far(rows):
    odd = lax.rem(lax.axis_index("rows"), 2)
    return (1 - odd) * (rows - 1), odd * (rows - 1)


def edges_kernel(values_ref, past_ref, near_ref, far_ref, near_past_ref, far_past_ref, sems):
    frames, rows = values_ref.shape[:2]
    lags = past_ref.shape[0]
    near, far = near_and_far(rows)
    late = pl.ds(frames - lags, lags)
    copies = [
        pltpu.make_async_copy(source, target, sems.at[index])
        for index, (source, target) in enumerate(
            (
                (values_ref.at[late], past_ref),
                (values_ref.at[:, near], near_ref),
                (values_ref.at[:, far], far_ref),
                (values_ref.at[late, near], near_past_ref),
                (values_ref.at[late, far], far_past_ref),
            )
        )
    ]
    for copy in copies:
        copy.start()
    for copy in copies:
        copy.wait()


def build_windows(body_of, edges_of, shape, mean, scale, offset, wide_ref):
    frames, rows, cols, chans = shape
    odd = lax.rem(lax.axis_index("rows"), 2) == 1
    has_past = lax.axis_index("frames") > 0
    has_above = lax.axis_index("rows") > 0
    has_below = lax.axis_index("rows") < lax.axis_size("rows") - 1
    column = lax.broadcasted_iota(jnp.int32, (cols, chans), 0)

    def put(frame, row, value, valid):
        value = (value.astype(jnp.float32) - mean) * scale + offset
        value = 0.5 * value * (1.0 + jnp.tanh(0.5 * value))
        if valid is not None:
            value = jnp.where(valid, value, 0.0)
        left = jnp.where(column == 0, 0.0, pltpu.roll(value, 1, 0))
        right = jnp.where(column == cols - 1, 0.0, pltpu.roll(value, cols - 1, 0))
        wide_ref[frame, row, :, 0:chans] = left.astype(jnp.bfloat16)
        wide_ref[frame, row, :, chans : 2 * chans] = value.astype(jnp.bfloat16)
        wide_ref[frame, row, :, 2 * chans :] = right.astype(jnp.bfloat16)

    def one(frame, valid):
        for row in range(rows):
            put(frame, row + 1, body_of(frame, row), valid)
        near, far = edges_of(frame)
        above = has_above if valid is None else jnp.logical_and(has_above, valid)
        below = has_below if valid is None else jnp.logical_and(has_below, valid)
        put(frame, 0, jnp.where(odd, near, far), above)
        put(frame, rows + 1, jnp.where(odd, far, near), below)

    return one, has_past


def conv_frames(wide_ref, kernel_ref, start, count, rows, cols, chans):
    total = None
    for lag_time in range(3):
        for lag_row in range(3):
            window = wide_ref[pl.ds(start + lag_time, count), lag_row : lag_row + rows]
            term = jnp.dot(
                window.reshape(count * rows * cols, 3 * chans),
                kernel_ref[lag_time, lag_row],
                preferred_element_type=jnp.float32,
            )
            total = term if total is None else total + term
    return total.reshape(count, rows, cols, -1)


def columns_apart(line, pair_ref):
    cols, chans = line.shape
    halves = range(chans // LANES)
    for half in halves:
        pair_ref[half] = line[:, half * LANES : (half + 1) * LANES]
    return (
        jnp.concatenate([pair_ref[half, pl.ds(k, cols // 2, stride=2)] for half in halves], axis=1)
        for k in range(2)
    )


def stats_kernel(values_ref, out_ref):
    local_stats(values_ref, 0, out_ref)


def first_kernel(
    own_ref, past_ref, near_ref, far_ref, near_past_ref, far_past_ref,
    stats_ref, gain_ref, offset_ref, kernel_ref,
    hidden_ref, out_stats_ref, out_near_ref, out_far_ref, wide_ref,
):
    frames, rows, cols, chans = own_ref.shape
    lags = past_ref.shape[0]
    count = frames * rows * cols * (chans // GROUPS)
    mean, scale = norm_terms(stats_ref, gain_ref, chans, count)
    terms = ((frames + lags, rows, cols, chans), mean, scale, offset_ref[...], wide_ref)
    put_past, has_past = build_windows(
        lambda f, r: past_ref[f, r], lambda f: (near_past_ref[f], far_past_ref[f]), *terms
    )
    put_own, _ = build_windows(
        lambda f, r: own_ref[f - lags, r], lambda f: (near_ref[f - lags], far_ref[f - lags]), *terms
    )

    def past(frame, carry):
        put_past(frame, has_past)
        return carry

    def own(frame, carry):
        put_own(frame, None)
        return carry

    lax.fori_loop(0, lags, past, 0)
    lax.fori_loop(lags, lags + frames, own, 0)
    step = 2
    near, far = near_and_far(rows)

    def some(index, carry):
        start = index * step
        conv = conv_frames(wide_ref, kernel_ref, start, step, rows, cols, chans)
        hidden_ref[pl.ds(start, step)] = conv.astype(jnp.bfloat16)
        return carry

    lax.fori_loop(0, (frames + 2) // step, some, 0)
    out_near_ref[...] = hidden_ref[:, near]
    out_far_ref[...] = hidden_ref[:, far]
    local_stats(hidden_ref, 2, out_stats_ref)


def second_kernel(
    hidden_ref, near_ref, far_ref, stats_ref, gain_ref, offset_ref, kernel_ref, source_ref,
    bias_ref, low_ref, high_ref, wide_ref, pair_ref,
):
    frames, rows, cols, chans = source_ref.shape
    count = frames * rows * cols * (chans // GROUPS)
    mean, scale = norm_terms(stats_ref, gain_ref, chans, count)
    put, has_past = build_windows(
        lambda f, r: hidden_ref[f, r], lambda f: (near_ref[f], far_ref[f]),
        hidden_ref.shape, mean, scale, offset_ref[...], wide_ref,
    )

    def past(frame, carry):
        put(frame, has_past)
        return carry

    def own(frame, carry):
        put(frame, None)
        return carry

    lax.fori_loop(0, 2, past, 0)
    lax.fori_loop(2, frames + 2, own, 0)
    factor = 0.5 ** 1.5
    bands = low_ref.shape[0]
    width = cols // 2 // bands

    def some(index, carry):
        start = index * 2
        conv = conv_frames(wide_ref, kernel_ref, start, 2, rows, cols, chans)
        summed = source_ref[pl.ds(start, 2)].astype(jnp.float32) + conv + bias_ref[...]
        for time_band in range(2):
            mixed = summed[0] - summed[1] if time_band else summed[0] + summed[1]
            for pair in range(rows // 2):
                upper, lower = mixed[2 * pair], mixed[2 * pair + 1]
                for row_band in range(2):
                    line = (upper - lower if row_band else upper + lower) * factor
                    even, uneven = columns_apart(line, pair_ref)
                    for col_band in range(2):
                        value = even - uneven if col_band else even + uneven
                        value = value.astype(jnp.bfloat16)
                        band = 4 * time_band + 2 * row_band + col_band
                        if band:
                            high_ref[band - 1, index, pair] = value
                        else:
                            for target in range(bands):
                                low_ref[target, index, pair] = value[
                                    target * width : (target + 1) * width
                                ]
        return carry

    lax.fori_loop(0, frames // 2, some, 0)


def routes():
    frame_count, row_count = lax.axis_size("frames"), lax.axis_size("rows")
    same = [(r, r) for r in range(row_count)]
    near = [(r, r ^ 1) for r in range(row_count)]
    far = [(r, ((r + 1) ^ 1) - 1) for r in range(1, row_count - 1)]

    def route(shift, pairs):
        return [
            (f * row_count + r, (f + shift) * row_count + s)
            for f in range(frame_count - shift)
            for r, s in pairs
        ]

    return route(0, near), route(0, far), route(1, same), route(1, near), route(1, far)


def send(values, route):
    return lax.ppermute(values, ("frames", "rows"), route)


def share(stats):
    return lax.all_to_all(stats, ("frames", "rows"), 0, 0, tiled=True)


def body(inputs, kernel_one, gain_one, offset_one, kernel_two, gain_two, offset_two, bias_two):
    frames, rows, cols, chans = inputs.shape
    devices = lax.axis_size("frames") * lax.axis_size("rows")
    bands = lax.axis_size("rows")
    lags = 4
    stats_shape = jax.ShapeDtypeStruct((devices, LANES), jnp.float32)
    weights_one = kernel_one.reshape(3, 3, 3 * chans, chans)
    weights_two = kernel_two.reshape(3, 3, 3 * chans, chans)

    def half(*shape):
        return jax.ShapeDtypeStruct(shape, jnp.bfloat16)

    def wide(count):
        return pltpu.VMEM((count, rows + 2, cols, 3 * chans), jnp.bfloat16)

    def call(kernel, name, mib, ins, out_shape, scratch=(), cost=None, space=VMEM):
        return pl.pallas_call(
            kernel, out_shape=out_shape, in_specs=[space] * len(ins),
            out_specs=jax.tree.map(lambda _: VMEM, out_shape), scratch_shapes=list(scratch),
            compiler_params=pltpu.CompilerParams(vmem_limit_bytes=mib * 2**20), name=name,
            cost_estimate=cost,
        )(*ins)

    to_near, to_far, to_next, to_next_near, to_next_far = routes()
    past, near, far, near_past, far_past = call(
        edges_kernel, "edges", 8, (inputs,),
        (
            half(lags, rows, cols, chans), half(frames, cols, chans), half(frames, cols, chans),
            half(lags, cols, chans), half(lags, cols, chans),
        ),
        [pltpu.SemaphoreType.DMA((5,))], space=pl.BlockSpec(memory_space=pl.ANY),
    )
    halos = (
        send(past, to_next), send(near, to_near), send(far, to_far),
        send(near_past, to_next_near), send(far_past, to_next_far),
    )
    stats = call(
        stats_kernel, "stats_one", 8, (inputs,), stats_shape,
        cost=pl.CostEstimate(flops=10**10, bytes_accessed=10**6, transcendentals=0),
    )
    stats = share(stats)
    hidden, stats, near, far = call(
        first_kernel, "conv_one", 32,
        (inputs, *halos, stats, gain_one[None], offset_one[None], weights_one),
        (
            half(frames + 2, rows, cols, chans), stats_shape,
            half(frames + 2, cols, chans), half(frames + 2, cols, chans),
        ),
        [wide(frames + lags)],
    )
    near, far = send(near, to_near), send(far, to_far)
    stats = share(stats)
    low, high = call(
        second_kernel, "conv_two", 32,
        (
            hidden, near, far, stats, gain_two[None], offset_two[None], weights_two, inputs,
            bias_two[None],
        ),
        (
            half(bands, frames // 2, rows // 2, cols // 2 // bands, chans),
            half(7, frames // 2, rows // 2, cols // 2, chans),
        ),
        [wide(frames + 2), pltpu.VMEM((chans // LANES, cols, LANES), jnp.float32)],
    )
    tiles = lax.all_to_all(low, "rows", split_axis=0, concat_axis=0, tiled=True)
    tiles = jnp.transpose(tiles, (1, 0, 2, 3, 4)).reshape(
        frames // 2, bands * (rows // 2), cols // 2 // bands, chans
    )
    return tiles, high


def solution(mesh):
    in_specs = (P("frames", "rows", None, None), P(), P(), P(), P(), P(), P(), P())
    out_specs = (P("frames", None, "rows", None), P(None, "frames", "rows", None, None))
    return jax.shard_map(body, mesh=mesh, in_specs=in_specs, out_specs=out_specs, check_vma=False)
```

```python
import functools

import jax
import jax.numpy as jnp
from jax import lax
from jax.experimental import pallas as pl
from jax.experimental.pallas import tpu as pltpu
from jax.sharding import PartitionSpec as P

GROUPS = 32
EPS = 1e-06
LANES = 128
LAGS = 4
VMEM = pl.BlockSpec(memory_space=pltpu.VMEM)
HBM = pl.BlockSpec(memory_space=pltpu.HBM)
HIGHEST = lax.Precision.HIGHEST


def exact_dot(left, right):
    return jnp.dot(left, right, precision=HIGHEST, preferred_element_type=jnp.float32)


def ties(rows, cols, row_is_channel, span, shifts):
    row = lax.broadcasted_iota(jnp.int32, (rows, cols), 0)
    col = lax.broadcasted_iota(jnp.int32, (rows, cols), 1)
    channel, lane = (row, col) if row_is_channel else (col, row)
    total = 0.0
    for shift in shifts:
        total = total + jnp.where(channel // span + shift == lane, 1.0, 0.0)
    return total


def to_lanes(sums):
    chans = sums.shape[1]
    matrix = ties(chans, LANES, True, chans // GROUPS, (0, GROUPS))
    return jnp.sum(exact_dot(sums, matrix), axis=0, keepdims=True)


def to_channels(lanes, chans, shifts):
    matrix = ties(LANES, chans, False, chans // GROUPS, shifts)
    return exact_dot(jnp.broadcast_to(lanes, (8, LANES)), matrix)[0:1]


def folded(values):
    return values.astype(jnp.float32).reshape(-1, 8, values.shape[-1])


def put_stats(out_ref, total, squares, centre, count):
    mean = to_lanes(total) / count
    away = mean - centre
    spread = to_lanes(squares) - count * (away * away)
    lane = lax.broadcasted_iota(jnp.int32, (1, LANES), 1)
    row = jnp.where(lane < GROUPS, mean, jnp.where(lane < 2 * GROUPS, spread, 0.0))
    out_ref[...] = jnp.broadcast_to(row, out_ref.shape)


def norm_terms(stats_ref, gain_ref, chans, count):
    stats = stats_ref[...]
    devices = stats.shape[0]
    average = jnp.sum(stats, axis=0, keepdims=True) / devices
    away = stats - average
    between = jnp.sum(away * away, axis=0, keepdims=True) / devices
    lane = lax.broadcasted_iota(jnp.int32, (1, LANES), 1)
    first = jnp.where(lane < GROUPS, average, 0.0)
    second = jnp.where(lane < GROUPS, between, jnp.where(lane < 2 * GROUPS, average / count, 0.0))
    mean = to_channels(first, chans, (0,))
    var = to_channels(second, chans, (0, GROUPS))
    return mean, gain_ref[...] / jnp.sqrt(var + EPS)


def near_and_far(rows):
    odd = lax.rem(lax.axis_index("rows"), 2)
    return (1 - odd) * (rows - 1), odd * (rows - 1)


def has_past():
    return lax.axis_index("frames") > 0


class Window:
    def __init__(self, wide_ref, mean, scale, offset):
        self.wide_ref = wide_ref
        self.terms = mean, scale, offset
        self.rows, self.cols = wide_ref.shape[1] - 2, wide_ref.shape[2]
        self.chans = wide_ref.shape[3] // 3
        place = lax.axis_index("rows")
        self.odd = lax.rem(place, 2) == 1
        self.above = place > 0
        self.below = place < lax.axis_size("rows") - 1
        self.column = lax.broadcasted_iota(jnp.int32, (self.cols, self.chans), 0)

    def put_row(self, frame, row, value, valid):
        mean, scale, offset = self.terms
        chans, cols = self.chans, self.cols
        value = (value.astype(jnp.float32) - mean) * scale + offset
        value = 0.5 * value * (1.0 + jnp.tanh(0.5 * value))
        if valid is not None:
            value = jnp.where(valid, value, 0.0)
        left = jnp.where(self.column == 0, 0.0, pltpu.roll(value, 1, 0))
        right = jnp.where(self.column == cols - 1, 0.0, pltpu.roll(value, cols - 1, 0))
        self.wide_ref[frame, row, :, 0:chans] = left.astype(jnp.bfloat16)
        self.wide_ref[frame, row, :, chans : 2 * chans] = value.astype(jnp.bfloat16)
        self.wide_ref[frame, row, :, 2 * chans :] = right.astype(jnp.bfloat16)

    def put(self, frame, body, near, far, valid):
        for row in range(self.rows):
            self.put_row(frame, row + 1, body[row], valid)
        above, below = self.above, self.below
        if valid is not None:
            above, below = jnp.logical_and(above, valid), jnp.logical_and(below, valid)
        self.put_row(frame, 0, jnp.where(self.odd, near, far), above)
        self.put_row(frame, self.rows + 1, jnp.where(self.odd, far, near), below)

    def conv(self, start, kernel_ref):
        total = None
        for lag_time in range(3):
            for lag_row in range(3):
                window = self.wide_ref[start + lag_time, lag_row : lag_row + self.rows]
                term = jnp.dot(
                    window.reshape(self.rows * self.cols, 3 * self.chans),
                    kernel_ref[lag_time, lag_row],
                    preferred_element_type=jnp.float32,
                )
                total = term if total is None else total + term
        return total


def edges_kernel(values_ref, past_ref, near_ref, far_ref, sems):
    frames, rows = values_ref.shape[:2]
    near, far = near_and_far(rows)
    pairs = (
        (values_ref.at[pl.ds(frames - LAGS, LAGS)], past_ref),
        (values_ref.at[:, near], near_ref),
        (values_ref.at[:, far], far_ref),
    )
    copies = [pltpu.make_async_copy(*pair, sems.at[i]) for i, pair in enumerate(pairs)]
    for copy in copies:
        copy.start()
    for copy in copies:
        copy.wait()


def past_edges_kernel(past_ref, near_ref, far_ref):
    near, far = near_and_far(past_ref.shape[1])
    near_ref[...] = past_ref[:, near]
    far_ref[...] = past_ref[:, far]


def stats_kernel(values_ref, out_ref):
    frames, rows, cols, chans = values_ref.shape
    count = float(frames * rows * cols * (chans // GROUPS))
    zero = jnp.zeros((8, chans), jnp.float32)

    def add(index, total):
        return total + jnp.sum(folded(values_ref[index]), axis=0)

    total = lax.fori_loop(0, frames, add, zero)
    lanes = to_lanes(total) / count
    centre = to_channels(lanes, chans, (0,))

    def add_square(index, total):
        away = folded(values_ref[index]) - centre
        return total + jnp.sum(away * away, axis=0)

    squares = lax.fori_loop(0, frames, add_square, zero)
    put_stats(out_ref, total, squares, lanes, count)


def group_count(frames, rows, cols, chans):
    return float(frames * rows * cols * (chans // GROUPS))


def first_kernel_own(
    own_ref, near_ref, far_ref, stats_ref, gain_ref, offset_ref, kernel_ref,
    hidden_ref, sums_ref, wide_ref,
):
    frames, rows, cols, chans = own_ref.shape
    mean, scale = norm_terms(stats_ref, gain_ref, chans, group_count(*own_ref.shape))
    window = Window(wide_ref, mean, scale, offset_ref[...])
    total = jnp.zeros((8, chans), jnp.float32)
    for frame in range(frames):
        window.put(frame, own_ref.at[frame], near_ref[frame], far_ref[frame], None)
        if frame < 2:
            continue
        hidden = window.conv(frame - 2, kernel_ref).astype(jnp.bfloat16)
        hidden_ref[frame - 2] = hidden.reshape(rows, cols, chans)
        total = total + jnp.sum(folded(hidden), axis=0)
    sums_ref[...] = total


def first_kernel_past(
    own_ref, near_ref, far_ref, past_ref, near_past_ref, far_past_ref,
    stats_ref, gain_ref, offset_ref, kernel_ref, later_ref, sums_ref,
    hidden_ref, out_stats_ref, out_near_ref, out_far_ref, wide_ref,
):
    frames, rows, cols, chans = own_ref.shape
    count = group_count(*own_ref.shape)
    mean, scale = norm_terms(stats_ref, gain_ref, chans, count)
    window = Window(wide_ref, mean, scale, offset_ref[...])
    sums = sums_ref[...]
    lanes = to_lanes(sums) / group_count(*later_ref.shape)
    centre = to_channels(lanes, chans, (0,))
    squares = jnp.zeros((8, chans), jnp.float32)
    later = 0
    for frame in range(LAGS + 2):
        own = frame - LAGS
        if own < 0:
            window.put(
                frame, past_ref.at[frame], near_past_ref[frame], far_past_ref[frame], has_past()
            )
        else:
            window.put(frame, own_ref.at[own], near_ref[own], far_ref[own], None)
        if frame < 2:
            continue
        hidden = window.conv(frame - 2, kernel_ref).astype(jnp.bfloat16)
        hidden_ref[frame - 2] = hidden.reshape(rows, cols, chans)
        blocks = [hidden] if own >= 0 else []
        while later * LAGS < later_ref.shape[0] * (frame - 1):
            blocks.append(later_ref[later])
            later += 1
        for block in blocks:
            away = folded(block) - centre
            squares = squares + jnp.sum(away * away, axis=0)
        if own >= 0:
            sums = sums + jnp.sum(folded(hidden), axis=0)
    put_stats(out_stats_ref, sums, squares, lanes, count)
    near, far = near_and_far(rows)
    for source, out_ref in ((near, out_near_ref), (far, out_far_ref)):
        out_ref[0:LAGS] = hidden_ref[:, source]
        out_ref[LAGS:] = later_ref[:, source]


def columns_apart(line, pair_ref):
    cols, chans = line.shape
    halves = range(chans // LANES)
    for half in halves:
        pair_ref[half] = line[:, half * LANES : (half + 1) * LANES]
    return (
        jnp.concatenate([pair_ref[half, pl.ds(k, cols // 2, stride=2)] for half in halves], axis=1)
        for k in range(2)
    )


def second_kernel(
    hidden_ref, later_ref, near_ref, far_ref, stats_ref, gain_ref, offset_ref, kernel_ref,
    source_ref, bias_ref, *rest,
):
    *low_refs, high_ref, wide_ref, pair_ref, low_ref, held_ref, sems = rest
    frames, rows, cols, chans = source_ref.shape
    mean, scale = norm_terms(stats_ref, gain_ref, chans, group_count(*source_ref.shape))
    window = Window(wide_ref, mean, scale, offset_ref[...])
    factor = 0.5**1.5
    bands = len(low_refs)
    width = cols // 2 // bands
    copies, summed = [], {}
    for frame in range(frames + 2):
        body = hidden_ref.at[frame] if frame < LAGS else later_ref.at[frame - LAGS]
        window.put(frame, body, near_ref[frame], far_ref[frame], has_past() if frame < 2 else None)
        if frame < 2:
            continue
        own = frame - 2
        conv = window.conv(own, kernel_ref).reshape(rows, cols, chans)
        summed[own % 2] = source_ref[own].astype(jnp.float32) + conv + bias_ref[...]
        if own % 2 == 0:
            continue
        index = own // 2
        for time_band in range(2):
            mixed = summed[0] - summed[1] if time_band else summed[0] + summed[1]
            for pair in range(rows // 2):
                upper, lower = mixed[2 * pair], mixed[2 * pair + 1]
                for row_band in range(2):
                    line = (upper - lower if row_band else upper + lower) * factor
                    slot = ((index * 2 + time_band) * (rows // 2) + pair) * 2 + row_band
                    even, uneven = columns_apart(line, pair_ref.at[slot % pair_ref.shape[0]])
                    for col_band in range(2):
                        value = even - uneven if col_band else even + uneven
                        value = value.astype(jnp.bfloat16)
                        band = 4 * time_band + 2 * row_band + col_band
                        if band:
                            held_ref[band - 1, index, pair] = value
                        else:
                            for target in range(bands):
                                low_ref[target, index, pair] = value[
                                    target * width : (target + 1) * width
                                ]
        copies.append(
            pltpu.make_async_copy(held_ref.at[:, index], high_ref.at[:, index], sems.at[index])
        )
        copies[-1].start()
    place = lax.axis_index("rows")
    for index, out_ref in enumerate(low_refs):
        out_ref[...] = low_ref[lax.bitwise_xor(place, index)]
    for copy in copies:
        copy.wait()


def low_kernel(*refs):
    *pieces, out_ref, sems = refs
    place = lax.axis_index("rows")
    rows = pieces[0].shape[1]
    copies = [
        pltpu.make_async_copy(
            piece, out_ref.at[:, pl.ds(lax.bitwise_xor(place, index) * rows, rows)], sems.at[index]
        )
        for index, piece in enumerate(pieces)
    ]
    for copy in copies:
        copy.start()
    for copy in copies:
        copy.wait()


def route(shift, pairs):
    frame_count, row_count = lax.axis_size("frames"), lax.axis_size("rows")
    return [
        (f * row_count + r, (f + shift) * row_count + s)
        for f in range(frame_count - shift)
        for r, s in pairs
    ]


def send(values, where):
    return lax.ppermute(values, ("frames", "rows"), where)


def share(stats):
    return lax.all_to_all(stats, ("frames", "rows"), 0, 0, tiled=True)


def half(*shape):
    return jax.ShapeDtypeStruct(shape, jnp.bfloat16)


def single(*shape):
    return jax.ShapeDtypeStruct(shape, jnp.float32)


def call(kernel, name, mib, ins, out_shape, scratch=(), cost=0, spaces=None, out_spaces=None):
    estimate = pl.CostEstimate(flops=cost, bytes_accessed=10**6, transcendentals=0)
    return pl.pallas_call(
        kernel,
        out_shape=out_shape,
        in_specs=spaces or [VMEM] * len(ins),
        out_specs=out_spaces or jax.tree.map(lambda _: VMEM, out_shape),
        scratch_shapes=list(scratch),
        compiler_params=pltpu.CompilerParams(vmem_limit_bytes=mib * 2**20),
        name=name,
        cost_estimate=estimate if cost else None,
    )(*ins)


def body(inputs, kernel_one, gain_one, offset_one, kernel_two, gain_two, offset_two, bias_two):
    frames, rows, cols, chans = inputs.shape
    bands = lax.axis_size("rows")
    devices = lax.axis_size("frames") * bands
    weights_one = kernel_one.reshape(3, 3, 3 * chans, chans)
    weights_two = kernel_two.reshape(3, 3, 3 * chans, chans)
    work = 2 * rows * cols * chans * 27 * chans
    to_near = route(0, [(r, r ^ 1) for r in range(bands)])
    to_far = route(0, [(r, ((r + 1) ^ 1) - 1) for r in range(1, bands - 1)])
    to_next = route(1, [(r, r) for r in range(bands)])

    def wide(count):
        return pltpu.VMEM((count, rows + 2, cols, 3 * chans), jnp.bfloat16)

    past, near, far = call(
        edges_kernel, "edges", 8, (inputs,),
        (half(LAGS, rows, cols, chans), half(frames, cols, chans), half(frames, cols, chans)),
        [pltpu.SemaphoreType.DMA((3,))], spaces=[HBM],
    )
    past, near, far = send(past, to_next), send(near, to_near), send(far, to_far)
    stats = call(stats_kernel, "stats_one", 8, (inputs,), single(devices, LANES), cost=10**10)
    stats = share(stats)
    near_past, far_past = call(
        past_edges_kernel, "past_edges", 8, (past,),
        (half(LAGS, cols, chans), half(LAGS, cols, chans)),
    )
    near_past, far_past = send(near_past, to_near), send(far_past, to_far)
    affine = (gain_one[None], offset_one[None])
    later, sums = call(
        first_kernel_own, "conv_one_own", 32,
        (inputs, near, far, stats, *affine, weights_one),
        (half(frames - 2, rows, cols, chans), single(8, chans)),
        [wide(frames)], cost=work * (frames - 2),
    )
    edge = half(frames + 2, cols, chans)
    hidden, stats, near, far = call(
        first_kernel_past, "conv_one_past", 32,
        (
            inputs, near, far, past, near_past, far_past, stats, *affine, weights_one, later, sums,
        ),
        (half(LAGS, rows, cols, chans), single(devices, LANES), edge, edge),
        [wide(LAGS + 2)], cost=work * LAGS,
    )
    near, far = send(near, to_near), send(far, to_far)
    stats = share(stats)
    piece = half(frames // 2, rows // 2, cols // 2 // bands, chans)
    high = half(7, frames // 2, rows // 2, cols // 2, chans)
    *pieces, high = call(
        second_kernel, "conv_two", 32,
        (
            hidden, later, near, far, stats, gain_two[None], offset_two[None], weights_two, inputs,
            bias_two[None],
        ),
        (*[piece] * bands, high),
        [
            wide(frames + 2), pltpu.VMEM((8, chans // LANES, cols, LANES), jnp.float32),
            pltpu.VMEM((bands, *piece.shape), jnp.bfloat16), pltpu.VMEM(high.shape, jnp.bfloat16),
            pltpu.SemaphoreType.DMA((frames // 2,)),
        ],
        cost=work * frames, out_spaces=(*[VMEM] * bands, HBM),
    )
    pieces = pieces[:1] + [
        send(pieces[k], route(0, [(r, r ^ k) for r in range(bands)])) for k in range(1, bands)
    ]
    low = call(
        low_kernel, "low_rows", 8, pieces,
        half(frames // 2, bands * (rows // 2), cols // 2 // bands, chans),
        [pltpu.SemaphoreType.DMA((bands,))], out_spaces=HBM,
    )
    return low, high


def solution(mesh):
    in_specs = (P("frames", "rows", None, None), P(), P(), P(), P(), P(), P(), P())
    out_specs = (P("frames", None, "rows", None), P(None, "frames", "rows", None, None))
    return jax.shard_map(body, mesh=mesh, in_specs=in_specs, out_specs=out_specs, check_vma=False)
```

```python
import functools

import jax
import jax.numpy as jnp
from jax import lax
from jax.experimental import pallas as pl
from jax.experimental.pallas import tpu as pltpu
from jax.sharding import PartitionSpec as P

GROUPS = 32
EPS = 1e-06
LANES = 128
LAGS = 4
STEP = 2
VMEM = pl.BlockSpec(memory_space=pltpu.VMEM)
HBM = pl.BlockSpec(memory_space=pltpu.HBM)


def group_sums(values):
    lane = lax.broadcasted_iota(jnp.int32, values.shape, 1)
    for bit in (1, 2, 4):
        partner = jnp.where(
            jnp.bitwise_and(lane, bit) == 0,
            pltpu.roll(values, LANES - bit, 1),
            pltpu.roll(values, bit, 1),
        )
        values = values + partner
    return values


def channel_group_sums(sums):
    sums = jnp.sum(sums, axis=0, keepdims=True)
    halves = [sums[:, at : at + LANES] for at in range(0, sums.shape[1], LANES)]
    return jnp.concatenate(
        [group_sums(jnp.broadcast_to(part, (8, LANES)))[0:1] for part in halves], axis=1
    )


def folded(values):
    return values.astype(jnp.float32).reshape(-1, 8, values.shape[-1])


def put_stats(out_ref, total, squares, centre, count):
    mean = channel_group_sums(total) / count
    away = mean - centre
    spread = channel_group_sums(squares) - count * (away * away)
    kind = jnp.bitwise_and(lax.broadcasted_iota(jnp.int32, (1, LANES), 1), 7)
    row = jnp.zeros((1, LANES), jnp.float32)
    for index, part in enumerate(
        (mean[:, :LANES], spread[:, :LANES], mean[:, LANES:], spread[:, LANES:])
    ):
        row = jnp.where(kind == index, part, row)
    out_ref[...] = jnp.broadcast_to(row, out_ref.shape)


def norm_terms(stats_ref, gain_ref, count):
    stats = stats_ref[...]
    devices = stats.shape[0]
    average = jnp.sum(stats, axis=0, keepdims=True) / devices
    away = stats - average
    between = jnp.sum(away * away, axis=0, keepdims=True) / devices
    within = average / count
    kind = jnp.bitwise_and(lax.broadcasted_iota(jnp.int32, (8, LANES), 1), 7)
    row = lax.broadcasted_iota(jnp.int32, (8, LANES), 0)
    terms = jnp.zeros((8, LANES), jnp.float32)
    for index, (lane, part) in enumerate(
        ((0, average), (2, average), (0, between), (2, between))
    ):
        terms = jnp.where(jnp.logical_and(row == index, kind == lane), part, terms)
    for index, lane in ((2, 1), (3, 3)):
        terms = jnp.where(jnp.logical_and(row == index, kind == lane), within, terms)
    terms = group_sums(terms)
    mean = jnp.concatenate([terms[0:1], terms[1:2]], axis=1)
    var = jnp.concatenate([terms[2:3], terms[3:4]], axis=1)
    return mean, gain_ref[...] / jnp.sqrt(var + EPS)


def near_and_far(rows):
    odd = lax.rem(lax.axis_index("rows"), 2)
    return (1 - odd) * (rows - 1), odd * (rows - 1)


def has_past():
    return lax.axis_index("frames") > 0


class Window:
    def __init__(self, wide_ref, mean, scale, offset, cols):
        self.wide_ref = wide_ref
        self.terms = mean, scale, offset
        self.cols, self.chans = cols, wide_ref.shape[3]
        self.pairs = wide_ref.shape[2] // cols
        self.rows = 2 * self.pairs
        place = lax.axis_index("rows")
        self.odd = lax.rem(place, 2) == 1
        self.above = place > 0
        self.below = place < lax.axis_size("rows") - 1

    def active(self, value, valid):
        mean, scale, offset = self.terms
        value = (value.astype(jnp.float32) - mean) * scale + offset
        value = 0.5 * value * (1.0 + jnp.tanh(0.5 * value))
        return value if valid is None else jnp.where(valid, value, 0.0)

    def put(self, frame, body, near, far, valid):
        above, below = self.above, self.below
        if valid is not None:
            above, below = jnp.logical_and(above, valid), jnp.logical_and(below, valid)
        lines = [self.active(jnp.where(self.odd, near, far), above)]
        lines += [self.active(body[row], valid) for row in range(self.rows)]
        lines += [self.active(jnp.where(self.odd, far, near), below)]
        for pair in range(self.pairs):
            first, second, third, fourth = lines[2 * pair : 2 * pair + 4]
            mixed = (
                first - third, 0.5 * (second + third), 0.5 * (third - second), second - fourth
            )
            for index, value in enumerate(mixed):
                self.wide_ref[frame, index, pair * self.cols : (pair + 1) * self.cols] = (
                    value.astype(jnp.bfloat16)
                )

    def conv(self, start, count, kernel_ref, mixed_ref, mix=False):
        shape = (count * self.pairs, self.cols, -1)
        column = lax.broadcasted_iota(jnp.int32, (1, self.cols, 1), 1)
        totals = [None, None]
        for lag_col in (1, 0, 2):
            if mix:
                mix_taps(kernel_ref, mixed_ref, lag_col)
            terms = []
            for index in range(4):
                window = jnp.concatenate(
                    [
                        self.wide_ref[start + lag : start + lag + count, index].reshape(
                            -1, self.chans
                        )
                        for lag in range(3)
                    ],
                    axis=1,
                )
                if index in (0, 3):
                    taps = [kernel_ref[lag, 2 * (index // 3), lag_col] for lag in range(3)]
                else:
                    taps = [mixed_ref[index - 1, lag, lag_col] for lag in range(3)]
                terms.append(
                    jnp.dot(
                        window, jnp.concatenate(taps, axis=0), preferred_element_type=jnp.float32
                    )
                )
            middle = terms[1] - terms[2]
            parts = terms[0] + (terms[1] + terms[2]), middle - terms[3]
            for at, part in enumerate(parts):
                part = part.reshape(shape)
                if lag_col == 0:
                    part = jnp.where(column == 0, 0.0, pltpu.roll(part, 1, 1))
                if lag_col == 2:
                    part = jnp.where(
                        column == self.cols - 1, 0.0, pltpu.roll(part, self.cols - 1, 1)
                    )
                totals[at] = part if totals[at] is None else totals[at] + part
        return [
            [totals[row % 2][frame * self.pairs + row // 2] for row in range(self.rows)]
            for frame in range(count)
        ]


def mix_taps(kernel_ref, mixed_ref, lag_col):
    for lag in range(3):
        first, second, third = (
            kernel_ref[lag, row, lag_col].astype(jnp.float32) for row in range(3)
        )
        outer = first + third
        mixed_ref[0, lag, lag_col] = (outer + second).astype(jnp.bfloat16)
        mixed_ref[1, lag, lag_col] = (outer - second).astype(jnp.bfloat16)


def edges_kernel(values_ref, past_ref, near_ref, far_ref, sems):
    frames, rows = values_ref.shape[:2]
    near, far = near_and_far(rows)
    pairs = (
        (values_ref.at[pl.ds(frames - LAGS, LAGS)], past_ref),
        (values_ref.at[:, near], near_ref),
        (values_ref.at[:, far], far_ref),
    )
    copies = [pltpu.make_async_copy(*pair, sems.at[i]) for i, pair in enumerate(pairs)]
    for copy in copies:
        copy.start()
    for copy in copies:
        copy.wait()


def past_edges_kernel(past_ref, near_ref, far_ref):
    near, far = near_and_far(past_ref.shape[1])
    near_ref[...] = past_ref[:, near]
    far_ref[...] = past_ref[:, far]


def stats_kernel(values_ref, out_ref):
    frames, rows, cols, chans = values_ref.shape
    count = float(frames * rows * cols * (chans // GROUPS))
    zero = jnp.zeros((8, chans), jnp.float32)

    def add(index, total):
        return total + jnp.sum(folded(values_ref[index]), axis=0)

    total = lax.fori_loop(0, frames, add, zero)
    centre = channel_group_sums(total) / count

    def add_square(index, total):
        away = folded(values_ref[index]) - centre
        return total + jnp.sum(away * away, axis=0)

    squares = lax.fori_loop(0, frames, add_square, zero)
    put_stats(out_ref, total, squares, centre, count)


def group_count(frames, rows, cols, chans):
    return float(frames * rows * cols * (chans // GROUPS))


def first_kernel_own(
    own_ref, near_ref, far_ref, stats_ref, gain_ref, offset_ref, kernel_ref,
    hidden_ref, sums_ref, mixed_ref, wide_ref,
):
    frames, rows, cols, chans = own_ref.shape
    mean, scale = norm_terms(stats_ref, gain_ref, group_count(*own_ref.shape))
    window = Window(wide_ref, mean, scale, offset_ref[...], cols)
    total = jnp.zeros((8, chans), jnp.float32)
    for frame in range(frames):
        window.put(frame, own_ref.at[frame], near_ref[frame], far_ref[frame], None)
        if frame < STEP + 1 or (frame - 1) % STEP:
            continue
        start = frame - 1 - STEP
        conv = window.conv(start, STEP, kernel_ref, mixed_ref, mix=start == 0)
        for at in range(STEP):
            for row in range(rows):
                hidden = conv[at][row].astype(jnp.bfloat16)
                hidden_ref[start + at, row] = hidden
                total = total + jnp.sum(folded(hidden), axis=0)
    sums_ref[...] = total


def first_kernel_past(
    own_ref, near_ref, far_ref, past_ref, near_past_ref, far_past_ref,
    stats_ref, gain_ref, offset_ref, kernel_ref, later_ref, sums_ref, mixed_ref,
    hidden_ref, out_stats_ref, out_near_ref, out_far_ref, wide_ref,
):
    frames, rows, cols, chans = own_ref.shape
    count = group_count(*own_ref.shape)
    mean, scale = norm_terms(stats_ref, gain_ref, count)
    window = Window(wide_ref, mean, scale, offset_ref[...], cols)
    sums = sums_ref[...]
    centre = channel_group_sums(sums) / group_count(*later_ref.shape)
    squares = jnp.zeros((8, chans), jnp.float32)

    def square(block):
        away = folded(block) - centre
        return jnp.sum(away * away, axis=0)

    for frame in range(LAGS + 2):
        own = frame - LAGS
        if own < 0:
            window.put(
                frame, past_ref.at[frame], near_past_ref[frame], far_past_ref[frame], has_past()
            )
        else:
            window.put(frame, own_ref.at[own], near_ref[own], far_ref[own], None)
        squares = squares + square(later_ref[frame])
        if frame < STEP + 1 or (frame - 1) % STEP:
            continue
        start = frame - 1 - STEP
        conv = window.conv(start, STEP, kernel_ref, mixed_ref)
        for at in range(STEP):
            for row in range(rows):
                hidden = conv[at][row].astype(jnp.bfloat16)
                hidden_ref[start + at, row] = hidden
                if start + at >= 2:
                    squares = squares + square(hidden)
                    sums = sums + jnp.sum(folded(hidden), axis=0)
    put_stats(out_stats_ref, sums, squares, centre, count)
    near, far = near_and_far(rows)
    for source, out_ref in ((near, out_near_ref), (far, out_far_ref)):
        out_ref[0:LAGS] = hidden_ref[:, source]
        out_ref[LAGS:] = later_ref[:, source]


def columns_apart(line, pair_ref):
    cols, chans = line.shape
    halves = range(chans // LANES)
    for half in halves:
        pair_ref[half] = line[:, half * LANES : (half + 1) * LANES]
    return (
        jnp.concatenate([pair_ref[half, pl.ds(k, cols // 2, stride=2)] for half in halves], axis=1)
        for k in range(2)
    )


def second_kernel(
    hidden_ref, later_ref, near_ref, far_ref, stats_ref, gain_ref, offset_ref, kernel_ref,
    source_ref, bias_ref, *rest,
):
    *low_refs, high_ref, wide_ref, mixed_ref, pair_ref, low_ref, held_ref, sems = rest
    frames, rows, cols, chans = source_ref.shape
    mean, scale = norm_terms(stats_ref, gain_ref, group_count(*source_ref.shape))
    window = Window(wide_ref, mean, scale, offset_ref[...], cols)
    factor = 0.5**1.5
    bands = len(low_refs)
    width = cols // 2 // bands
    copies = []
    for frame in range(frames + 2):
        body = hidden_ref.at[frame] if frame < LAGS else later_ref.at[frame - LAGS]
        window.put(frame, body, near_ref[frame], far_ref[frame], has_past() if frame < 2 else None)
        if frame < 3 or frame % 2 == 0:
            continue
        start = frame - 3
        index = start // 2
        conv = window.conv(start, 2, kernel_ref, mixed_ref, mix=start == 0)
        summed = [
            [
                source_ref[start + at, row].astype(jnp.float32) + conv[at][row] + bias_ref[...]
                for row in range(rows)
            ]
            for at in range(2)
        ]
        for time_band in range(2):
            mixed = [
                before - after if time_band else before + after
                for before, after in zip(*summed, strict=True)
            ]
            for pair in range(rows // 2):
                upper, lower = mixed[2 * pair], mixed[2 * pair + 1]
                for row_band in range(2):
                    line = (upper - lower if row_band else upper + lower) * factor
                    slot = ((index * 2 + time_band) * (rows // 2) + pair) * 2 + row_band
                    even, uneven = columns_apart(line, pair_ref.at[slot % pair_ref.shape[0]])
                    for col_band in range(2):
                        value = even - uneven if col_band else even + uneven
                        value = value.astype(jnp.bfloat16)
                        band = 4 * time_band + 2 * row_band + col_band
                        if band:
                            held_ref[band - 1, index, pair] = value
                        else:
                            for target in range(bands):
                                low_ref[target, index, pair] = value[
                                    target * width : (target + 1) * width
                                ]
        copies.append(
            pltpu.make_async_copy(held_ref.at[:, index], high_ref.at[:, index], sems.at[index])
        )
        copies[-1].start()
    place = lax.axis_index("rows")
    for index, out_ref in enumerate(low_refs):
        out_ref[...] = low_ref[lax.bitwise_xor(place, index)]
    for copy in copies:
        copy.wait()


def low_kernel(*refs):
    *pieces, out_ref, sems = refs
    place = lax.axis_index("rows")
    rows = pieces[0].shape[1]
    copies = [
        pltpu.make_async_copy(
            piece, out_ref.at[:, pl.ds(lax.bitwise_xor(place, index) * rows, rows)], sems.at[index]
        )
        for index, piece in enumerate(pieces)
    ]
    for copy in copies:
        copy.start()
    for copy in copies:
        copy.wait()


def route(shift, pairs):
    frame_count, row_count = lax.axis_size("frames"), lax.axis_size("rows")
    return [
        (f * row_count + r, (f + shift) * row_count + s)
        for f in range(frame_count - shift)
        for r, s in pairs
    ]


def send(values, where):
    return lax.ppermute(values, ("frames", "rows"), where)


def share(stats):
    return lax.all_to_all(stats, ("frames", "rows"), 0, 0, tiled=True)


def half(*shape):
    return jax.ShapeDtypeStruct(shape, jnp.bfloat16)


def single(*shape):
    return jax.ShapeDtypeStruct(shape, jnp.float32)


def call(kernel, name, mib, ins, out_shape, scratch=(), cost=0, spaces=None, out_spaces=None):
    estimate = pl.CostEstimate(flops=cost, bytes_accessed=10**6, transcendentals=0)
    return pl.pallas_call(
        kernel,
        out_shape=out_shape,
        in_specs=spaces or [VMEM] * len(ins),
        out_specs=out_spaces or jax.tree.map(lambda _: VMEM, out_shape),
        scratch_shapes=list(scratch),
        compiler_params=pltpu.CompilerParams(vmem_limit_bytes=mib * 2**20),
        name=name,
        cost_estimate=estimate if cost else None,
    )(*ins)


def body(inputs, kernel_one, gain_one, offset_one, kernel_two, gain_two, offset_two, bias_two):
    frames, rows, cols, chans = inputs.shape
    bands = lax.axis_size("rows")
    devices = lax.axis_size("frames") * bands
    work = 2 * rows * cols * chans * 18 * chans
    to_near = route(0, [(r, r ^ 1) for r in range(bands)])
    to_far = route(0, [(r, ((r + 1) ^ 1) - 1) for r in range(1, bands - 1)])
    to_next = route(1, [(r, r) for r in range(bands)])

    def wide(count):
        return pltpu.VMEM((count, 4, rows // 2 * cols, chans), jnp.bfloat16)

    past, near, far = call(
        edges_kernel, "edges", 8, (inputs,),
        (half(LAGS, rows, cols, chans), half(frames, cols, chans), half(frames, cols, chans)),
        [pltpu.SemaphoreType.DMA((3,))], spaces=[HBM],
    )
    past, near, far = send(past, to_next), send(near, to_near), send(far, to_far)
    stats = call(stats_kernel, "stats_one", 8, (inputs,), single(devices, LANES), cost=10**10)
    past, stats = lax.optimization_barrier((past, share(stats)))
    near_past, far_past = call(
        past_edges_kernel, "past_edges", 8, (past,),
        (half(LAGS, cols, chans), half(LAGS, cols, chans)),
    )
    near_past, far_past = send(near_past, to_near), send(far_past, to_far)
    affine = (gain_one[None], offset_one[None])
    mixed = half(2, 3, 3, chans, chans)
    later, sums, mixed_one = call(
        first_kernel_own, "conv_one_own", 32,
        (inputs, near, far, stats, *affine, kernel_one),
        (half(frames - 2, rows, cols, chans), single(8, chans), mixed),
        [wide(frames)], cost=work * (frames - 2),
    )
    edge = half(frames + 2, cols, chans)
    hidden, stats, near, far = call(
        first_kernel_past, "conv_one_past", 32,
        (
            inputs, near, far, past, near_past, far_past, stats, *affine, kernel_one, later, sums,
            mixed_one,
        ),
        (half(LAGS, rows, cols, chans), single(devices, LANES), edge, edge),
        [wide(LAGS + 2)], cost=work * LAGS,
    )
    near, far = send(near, to_near), send(far, to_far)
    stats = share(stats)
    piece = half(frames // 2, rows // 2, cols // 2 // bands, chans)
    high = half(7, frames // 2, rows // 2, cols // 2, chans)
    *pieces, high = call(
        second_kernel, "conv_two", 32,
        (
            hidden, later, near, far, stats, gain_two[None], offset_two[None], kernel_two, inputs,
            bias_two[None],
        ),
        (*[piece] * bands, high),
        [
            wide(frames + 2), pltpu.VMEM(mixed.shape, jnp.bfloat16), pltpu.VMEM((8, chans // LANES, cols, LANES), jnp.float32),
            pltpu.VMEM((bands, *piece.shape), jnp.bfloat16), pltpu.VMEM(high.shape, jnp.bfloat16),
            pltpu.SemaphoreType.DMA((frames // 2,)),
        ],
        cost=work * frames, out_spaces=(*[VMEM] * bands, HBM),
    )
    pieces = pieces[:1] + [
        send(pieces[k], route(0, [(r, r ^ k) for r in range(bands)])) for k in range(1, bands)
    ]
    low = call(
        low_kernel, "low_rows", 8, pieces,
        half(frames // 2, bands * (rows // 2), cols // 2 // bands, chans),
        [pltpu.SemaphoreType.DMA((bands,))], out_spaces=HBM,
    )
    return low, high


def solution(mesh):
    in_specs = (P("frames", "rows", None, None), P(), P(), P(), P(), P(), P(), P())
    out_specs = (P("frames", None, "rows", None), P(None, "frames", "rows", None, None))
    return jax.shard_map(body, mesh=mesh, in_specs=in_specs, out_specs=out_specs, check_vma=False)
```

```python
import functools

import jax
import jax.numpy as jnp
from jax import lax
from jax.experimental import pallas as pl
from jax.experimental.pallas import tpu as pltpu
from jax.sharding import PartitionSpec as P

GROUPS = 32
EPS = 1e-06
LANES = 128
LAGS = 4
STEP = 2
LAG_COLS = (1, 0, 2)
VMEM = pl.BlockSpec(memory_space=pltpu.VMEM)
HBM = pl.BlockSpec(memory_space=pltpu.HBM)


def group_sums(values):
    lane = lax.broadcasted_iota(jnp.int32, values.shape, 1)
    for bit in (1, 2, 4):
        partner = jnp.where(
            jnp.bitwise_and(lane, bit) == 0,
            pltpu.roll(values, LANES - bit, 1),
            pltpu.roll(values, bit, 1),
        )
        values = values + partner
    return values


def channel_group_sums(sums):
    sums = jnp.sum(sums, axis=0, keepdims=True)
    halves = [sums[:, at : at + LANES] for at in range(0, sums.shape[1], LANES)]
    return jnp.concatenate(
        [group_sums(jnp.broadcast_to(part, (8, LANES)))[0:1] for part in halves], axis=1
    )


def folded(values):
    return values.astype(jnp.float32).reshape(-1, 8, values.shape[-1])


def put_stats(out_ref, total, squares, centre, count):
    mean = channel_group_sums(total) / count
    away = mean - centre
    spread = channel_group_sums(squares) - count * (away * away)
    kind = jnp.bitwise_and(lax.broadcasted_iota(jnp.int32, (1, LANES), 1), 7)
    row = jnp.zeros((1, LANES), jnp.float32)
    for index, part in enumerate(
        (mean[:, :LANES], spread[:, :LANES], mean[:, LANES:], spread[:, LANES:])
    ):
        row = jnp.where(kind == index, part, row)
    out_ref[...] = jnp.broadcast_to(row, out_ref.shape)


def norm_terms(stats_ref, gain_ref, count):
    stats = stats_ref[...]
    devices = stats.shape[0]
    average = jnp.sum(stats, axis=0, keepdims=True) / devices
    away = stats - average
    between = jnp.sum(away * away, axis=0, keepdims=True) / devices
    within = average / count
    kind = jnp.bitwise_and(lax.broadcasted_iota(jnp.int32, (8, LANES), 1), 7)
    row = lax.broadcasted_iota(jnp.int32, (8, LANES), 0)
    terms = jnp.zeros((8, LANES), jnp.float32)
    for index, (lane, part) in enumerate(
        ((0, average), (2, average), (0, between), (2, between))
    ):
        terms = jnp.where(jnp.logical_and(row == index, kind == lane), part, terms)
    for index, lane in ((2, 1), (3, 3)):
        terms = jnp.where(jnp.logical_and(row == index, kind == lane), within, terms)
    terms = group_sums(terms)
    mean = jnp.concatenate([terms[0:1], terms[1:2]], axis=1)
    var = jnp.concatenate([terms[2:3], terms[3:4]], axis=1)
    return mean, gain_ref[...] / jnp.sqrt(var + EPS)


def near_and_far(rows):
    odd = lax.rem(lax.axis_index("rows"), 2)
    return (1 - odd) * (rows - 1), odd * (rows - 1)


def row_place():
    place = lax.axis_index("rows")
    return lax.rem(place, 2) == 1, place > 0, place < lax.axis_size("rows") - 1


def has_past():
    return lax.axis_index("frames") > 0


def active(value, terms, valid):
    mean, scale, offset = terms
    value = (value.astype(jnp.float32) - mean) * scale + offset
    value = 0.5 * value * (1.0 + jnp.tanh(0.5 * value))
    return value if valid is None else jnp.where(valid, value, 0.0)


class Window:
    def __init__(self, wide_ref, mean, scale, offset, cols):
        self.wide_ref = wide_ref
        self.terms = mean, scale, offset
        self.cols, self.chans = cols, wide_ref.shape[3]
        self.pairs = wide_ref.shape[2] // cols
        self.rows = 2 * self.pairs
        self.odd, self.above, self.below = row_place()

    def active(self, value, valid):
        return active(value, self.terms, valid)

    def put(self, frame, body, near, far, valid):
        above, below = self.above, self.below
        if valid is not None:
            above, below = jnp.logical_and(above, valid), jnp.logical_and(below, valid)
        lines = [self.active(jnp.where(self.odd, near, far), above)]
        lines += [self.active(body[row], valid) for row in range(self.rows)]
        lines += [self.active(jnp.where(self.odd, far, near), below)]
        for pair in range(self.pairs):
            first, second, third, fourth = lines[2 * pair : 2 * pair + 4]
            mixed = (
                first - third, 0.5 * (second + third), 0.5 * (third - second), second - fourth
            )
            for index, value in enumerate(mixed):
                self.wide_ref[frame, index, pair * self.cols : (pair + 1) * self.cols] = (
                    value.astype(jnp.bfloat16)
                )

    def conv(self, start, count, kernel_ref, mixed_ref, mix=False):
        totals = [None, None]
        for lag_col in LAG_COLS:
            if mix:
                mix_taps(kernel_ref, mixed_ref, lag_col)
            terms = []
            for index in range(4):
                if index in (0, 3):
                    taps = [kernel_ref[lag, 2 * (index // 3), lag_col] for lag in range(3)]
                else:
                    taps = [mixed_ref[index - 1, lag, lag_col] for lag in range(3)]
                terms.append(product(self.wide_ref, start, count, index, taps))
            middle = terms[1] - terms[2]
            parts = terms[0] + (terms[1] + terms[2]), middle - terms[3]
            for at, part in enumerate(parts):
                part = shifted(part, self.cols, lag_col)
                totals[at] = part if totals[at] is None else totals[at] + part
        return [
            [totals[row % 2][frame * self.pairs + row // 2] for row in range(self.rows)]
            for frame in range(count)
        ]


def product(wide_ref, start, count, index, taps):
    window = jnp.concatenate(
        [
            wide_ref[start + lag : start + lag + count, index].reshape(-1, wide_ref.shape[3])
            for lag in range(3)
        ],
        axis=1,
    )
    return jnp.dot(window, jnp.concatenate(taps, axis=0), preferred_element_type=jnp.float32)


def shifted(part, cols, lag_col):
    part = part.reshape(-1, cols, part.shape[-1])
    column = lax.broadcasted_iota(jnp.int32, (1, cols, 1), 1)
    if lag_col == 0:
        part = jnp.where(column == 0, 0.0, pltpu.roll(part, 1, 1))
    if lag_col == 2:
        part = jnp.where(column == cols - 1, 0.0, pltpu.roll(part, cols - 1, 1))
    return part


def mix_taps(kernel_ref, mixed_ref, lag_col):
    for lag in range(3):
        first, second, third = (
            kernel_ref[lag, row, lag_col].astype(jnp.float32) for row in range(3)
        )
        outer = first + third
        mixed_ref[0, lag, lag_col] = (outer + second).astype(jnp.bfloat16)
        mixed_ref[1, lag, lag_col] = (outer - second).astype(jnp.bfloat16)


def past_kernel(values_ref, past_ref):
    past_ref[...] = values_ref[values_ref.shape[0] - LAGS :]


def edges_kernel(values_ref, past_ref, near_ref, far_ref):
    near, far = near_and_far(values_ref.shape[1])
    for row, out_ref in ((near, near_ref), (far, far_ref)):
        out_ref[0:LAGS] = past_ref[:, row]
        out_ref[LAGS:] = values_ref[:, row]


def stats_kernel(values_ref, out_ref):
    frames, rows, cols, chans = values_ref.shape
    count = float(frames * rows * cols * (chans // GROUPS))
    zero = jnp.zeros((8, chans), jnp.float32)

    def add(index, total):
        return total + jnp.sum(folded(values_ref[index]), axis=0)

    total = lax.fori_loop(0, frames, add, zero)
    centre = channel_group_sums(total) / count

    def add_square(index, total):
        away = folded(values_ref[index]) - centre
        return total + jnp.sum(away * away, axis=0)

    squares = lax.fori_loop(0, frames, add_square, zero)
    put_stats(out_ref, total, squares, centre, count)


def group_count(frames, rows, cols, chans):
    return float(frames * rows * cols * (chans // GROUPS))


def inner_kernel(
    own_ref, past_ref, stats_ref, gain_ref, offset_ref, kernel_ref,
    hidden_ref, partial_ref, middle_ref, sums_ref, wide_ref, side_ref, mixed_ref,
):
    frames, rows, cols, chans = own_ref.shape
    terms = (*norm_terms(stats_ref, gain_ref, group_count(*own_ref.shape)), offset_ref[...])
    total = jnp.zeros((8, chans), jnp.float32)
    for frame in range(frames + LAGS):
        body, valid = own_ref.at[frame - LAGS], None
        if frame < LAGS:
            body, valid = past_ref.at[frame], has_past()
        lines = [active(body[row], terms, valid) for row in range(rows)]
        for pair in range(2):
            first, second = lines[2 * pair : 2 * pair + 2]
            for index, value in enumerate((0.5 * (first + second), 0.5 * (second - first))):
                wide_ref[frame, index, pair * cols : (pair + 1) * cols] = value.astype(jnp.bfloat16)
            side_ref[frame, pair] = (lines[pair] - lines[pair + 2]).astype(jnp.bfloat16)
            middle_ref[frame, pair] = lines[pair + 1].astype(jnp.bfloat16)
        if frame < STEP + 1 or (frame - 1) % STEP:
            continue
        start = frame - 1 - STEP
        sums = [None, None]
        sides = [None, None]
        for lag_col in LAG_COLS:
            if start == 0:
                mix_taps(kernel_ref, mixed_ref, lag_col)
            taps = [[mixed_ref[at, lag, lag_col] for lag in range(3)] for at in range(2)]
            plus, minus = (product(wide_ref, start, STEP, at, taps[at]) for at in range(2))
            for at, part in enumerate((plus + minus, plus - minus)):
                part = shifted(part, cols, lag_col)
                sums[at] = part if sums[at] is None else sums[at] + part
            for at in range(2):
                taps = [kernel_ref[lag, 2 - 2 * at, lag_col] for lag in range(3)]
                part = shifted(product(side_ref, start, STEP, at, taps), cols, lag_col)
                sides[at] = part if sides[at] is None else sides[at] + part
        for at in range(STEP):
            place = start + at
            partial_ref[place, 0] = sums[0][2 * at]
            partial_ref[place, 1] = sums[1][2 * at + 1]
            for row, value in enumerate(
                (sums[1][2 * at] - sides[0][at], sums[0][2 * at + 1] + sides[1][at])
            ):
                hidden = value.astype(jnp.bfloat16)
                hidden_ref[place, row] = hidden
                if place >= 2:
                    total = total + jnp.sum(folded(hidden), axis=0)
    sums_ref[...] = total


def outer_kernel(
    near_ref, far_ref, stats_ref, gain_ref, offset_ref, kernel_ref,
    hidden_ref, partial_ref, middle_ref, sums_ref,
    out_stats_ref, out_near_ref, out_far_ref, side_ref,
):
    count_frames, rows, cols, chans = hidden_ref.shape
    frames = count_frames - 2
    count = group_count(frames, 2 * rows, cols, chans)
    terms = (*norm_terms(stats_ref, gain_ref, count), offset_ref[...])
    odd, above, below = row_place()
    sums = sums_ref[...]
    centre = channel_group_sums(sums) / (count / 2)
    squares = jnp.zeros((8, chans), jnp.float32)

    def square(block):
        away = folded(block) - centre
        return jnp.sum(away * away, axis=0)

    for frame in range(frames + LAGS):
        valids = above, below
        if frame < LAGS:
            valids = [jnp.logical_and(valid, has_past()) for valid in valids]
        near, far = near_ref[frame], far_ref[frame]
        upper = active(jnp.where(odd, near, far), terms, valids[0])
        lower = active(jnp.where(odd, far, near), terms, valids[1])
        middle = [middle_ref[frame, row].astype(jnp.float32) for row in range(2)]
        side_ref[frame, 0] = (upper - middle[0]).astype(jnp.bfloat16)
        side_ref[frame, 1] = (middle[1] - lower).astype(jnp.bfloat16)
        if 2 <= frame < count_frames:
            squares = squares + square(hidden_ref[frame])
        if frame < STEP + 1 or (frame - 1) % STEP:
            continue
        start = frame - 1 - STEP
        sides = [None, None]
        for lag_col in LAG_COLS:
            for at in range(2):
                taps = [kernel_ref[lag, 2 * at, lag_col] for lag in range(3)]
                part = shifted(product(side_ref, start, STEP, at, taps), cols, lag_col)
                sides[at] = part if sides[at] is None else sides[at] + part
        for at in range(STEP):
            place = start + at
            edges = [
                (partial_ref[place, 0] + sides[0][at]).astype(jnp.bfloat16),
                (partial_ref[place, 1] - sides[1][at]).astype(jnp.bfloat16),
            ]
            out_near_ref[place] = jnp.where(odd, edges[0], edges[1])
            out_far_ref[place] = jnp.where(odd, edges[1], edges[0])
            if place >= 2:
                for edge in edges:
                    squares = squares + square(edge)
                    sums = sums + jnp.sum(folded(edge), axis=0)
    put_stats(out_stats_ref, sums, squares, centre, count)


def columns_apart(line, pair_ref):
    cols, chans = line.shape
    halves = range(chans // LANES)
    for half in halves:
        pair_ref[half] = line[:, half * LANES : (half + 1) * LANES]
    return (
        jnp.concatenate([pair_ref[half, pl.ds(k, cols // 2, stride=2)] for half in halves], axis=1)
        for k in range(2)
    )


def second_kernel(
    hidden_ref, own_near_ref, own_far_ref, near_ref, far_ref, stats_ref, gain_ref, offset_ref,
    kernel_ref, source_ref, bias_ref, *rest,
):
    *low_refs, high_ref, wide_ref, mixed_ref, pair_ref, low_ref, held_ref, sems = rest
    frames, rows, cols, chans = source_ref.shape
    mean, scale = norm_terms(stats_ref, gain_ref, group_count(*source_ref.shape))
    window = Window(wide_ref, mean, scale, offset_ref[...], cols)
    factor = 0.5**1.5
    bands = len(low_refs)
    width = cols // 2 // bands
    copies = []
    for frame in range(frames + 2):
        near, far = own_near_ref[frame], own_far_ref[frame]
        body = (
            jnp.where(window.odd, near, far), hidden_ref[frame, 0], hidden_ref[frame, 1],
            jnp.where(window.odd, far, near),
        )
        window.put(frame, body, near_ref[frame], far_ref[frame], has_past() if frame < 2 else None)
        if frame < 3 or frame % 2 == 0:
            continue
        start = frame - 3
        index = start // 2
        conv = window.conv(start, 2, kernel_ref, mixed_ref, mix=start == 0)
        summed = [
            [
                source_ref[start + at, row].astype(jnp.float32) + conv[at][row] + bias_ref[...]
                for row in range(rows)
            ]
            for at in range(2)
        ]
        for time_band in range(2):
            mixed = [
                before - after if time_band else before + after
                for before, after in zip(*summed, strict=True)
            ]
            for pair in range(rows // 2):
                upper, lower = mixed[2 * pair], mixed[2 * pair + 1]
                for row_band in range(2):
                    line = (upper - lower if row_band else upper + lower) * factor
                    slot = ((index * 2 + time_band) * (rows // 2) + pair) * 2 + row_band
                    even, uneven = columns_apart(line, pair_ref.at[slot % pair_ref.shape[0]])
                    for col_band in range(2):
                        value = even - uneven if col_band else even + uneven
                        value = value.astype(jnp.bfloat16)
                        band = 4 * time_band + 2 * row_band + col_band
                        if band:
                            held_ref[band - 1, index, pair] = value
                        else:
                            for target in range(bands):
                                low_ref[target, index, pair] = value[
                                    target * width : (target + 1) * width
                                ]
        copies.append(
            pltpu.make_async_copy(held_ref.at[:, index], high_ref.at[:, index], sems.at[index])
        )
        copies[-1].start()
    place = lax.axis_index("rows")
    for index, out_ref in enumerate(low_refs):
        out_ref[...] = low_ref[lax.bitwise_xor(place, index)]
    for copy in copies:
        copy.wait()


def low_kernel(*refs):
    *pieces, out_ref, sems = refs
    place = lax.axis_index("rows")
    rows = pieces[0].shape[1]
    copies = [
        pltpu.make_async_copy(
            piece, out_ref.at[:, pl.ds(lax.bitwise_xor(place, index) * rows, rows)], sems.at[index]
        )
        for index, piece in enumerate(pieces)
    ]
    for copy in copies:
        copy.start()
    for copy in copies:
        copy.wait()


def route(shift, pairs):
    frame_count, row_count = lax.axis_size("frames"), lax.axis_size("rows")
    return [
        (f * row_count + r, (f + shift) * row_count + s)
        for f in range(frame_count - shift)
        for r, s in pairs
    ]


def send(values, where):
    return lax.ppermute(values, ("frames", "rows"), where)


def share(stats):
    return lax.all_to_all(stats, ("frames", "rows"), 0, 0, tiled=True)


def half(*shape):
    return jax.ShapeDtypeStruct(shape, jnp.bfloat16)


def single(*shape):
    return jax.ShapeDtypeStruct(shape, jnp.float32)


def call(kernel, name, mib, ins, out_shape, scratch=(), cost=0, spaces=None, out_spaces=None):
    estimate = pl.CostEstimate(flops=cost, bytes_accessed=10**6, transcendentals=0)
    return pl.pallas_call(
        kernel,
        out_shape=out_shape,
        in_specs=spaces or [VMEM] * len(ins),
        out_specs=out_spaces or jax.tree.map(lambda _: VMEM, out_shape),
        scratch_shapes=list(scratch),
        compiler_params=pltpu.CompilerParams(vmem_limit_bytes=mib * 2**20),
        name=name,
        cost_estimate=estimate if cost else None,
    )(*ins)


def body(inputs, kernel_one, gain_one, offset_one, kernel_two, gain_two, offset_two, bias_two):
    frames, rows, cols, chans = inputs.shape
    bands = lax.axis_size("rows")
    devices = lax.axis_size("frames") * bands
    work = 2 * rows * cols * chans * 18 * chans
    to_near = route(0, [(r, r ^ 1) for r in range(bands)])
    to_far = route(0, [(r, ((r + 1) ^ 1) - 1) for r in range(1, bands - 1)])
    to_next = route(1, [(r, r) for r in range(bands)])

    def window(*shape):
        return pltpu.VMEM(shape, jnp.bfloat16)

    past = call(past_kernel, "past", 8, (inputs,), half(LAGS, rows, cols, chans))
    past = send(past, to_next)
    stats = call(stats_kernel, "stats_one", 8, (inputs,), single(devices, LANES), cost=10**10)
    past, stats = lax.optimization_barrier((past, share(stats)))
    reach = frames + LAGS
    near, far = call(
        edges_kernel, "edges", 8, (inputs, past),
        (half(reach, cols, chans), half(reach, cols, chans)),
    )
    near, far = send(near, to_near), send(far, to_far)
    affine = (gain_one[None], offset_one[None])
    inner, partial, middle, sums = call(
        inner_kernel, "conv_inner", 32, (inputs, past, stats, *affine, kernel_one),
        (
            half(frames + 2, 2, cols, chans), single(frames + 2, 2, cols, chans),
            half(reach, 2, cols, chans), single(8, chans),
        ),
        [
            window(reach, 2, 2 * cols, chans), window(reach, 2, cols, chans),
            window(2, 3, 3, chans, chans),
        ],
        cost=work * (frames + 2),
    )
    edge = half(frames + 2, cols, chans)
    stats, own_near, own_far = call(
        outer_kernel, "conv_outer", 32,
        (near, far, stats, *affine, kernel_one, inner, partial, middle, sums),
        (single(devices, LANES), edge, edge), [window(reach, 2, cols, chans)], cost=work * 4,
    )
    near, far = send(own_near, to_near), send(own_far, to_far)
    stats = share(stats)
    piece = half(frames // 2, rows // 2, cols // 2 // bands, chans)
    high = half(7, frames // 2, rows // 2, cols // 2, chans)
    *pieces, high = call(
        second_kernel, "conv_two", 32,
        (
            inner, own_near, own_far, near, far, stats, gain_two[None], offset_two[None], kernel_two, inputs,
            bias_two[None],
        ),
        (*[piece] * bands, high),
        [
            window(frames + 2, 4, rows // 2 * cols, chans), window(2, 3, 3, chans, chans),
            pltpu.VMEM((8, chans // LANES, cols, LANES), jnp.float32),
            window(bands, *piece.shape), window(*high.shape),
            pltpu.SemaphoreType.DMA((frames // 2,)),
        ],
        cost=work * frames, out_spaces=(*[VMEM] * bands, HBM),
    )
    pieces = pieces[:1] + [
        send(pieces[k], route(0, [(r, r ^ k) for r in range(bands)])) for k in range(1, bands)
    ]
    low = call(
        low_kernel, "low_rows", 8, pieces,
        half(frames // 2, bands * (rows // 2), cols // 2 // bands, chans),
        [pltpu.SemaphoreType.DMA((bands,))], out_spaces=HBM,
    )
    return low, high


def solution(mesh):
    in_specs = (P("frames", "rows", None, None), P(), P(), P(), P(), P(), P(), P())
    out_specs = (P("frames", None, "rows", None), P(None, "frames", "rows", None, None))
    return jax.shard_map(body, mesh=mesh, in_specs=in_specs, out_specs=out_specs, check_vma=False)
```

```python
import functools

import jax
import jax.numpy as jnp
from jax import lax
from jax.experimental import pallas as pl
from jax.experimental.pallas import tpu as pltpu
from jax.sharding import PartitionSpec as P

GROUPS = 32
EPS = 1e-06
LANES = 128
LAGS = 4
STEP = 2
LAG_COLS = (1, 0, 2)
VMEM = pl.BlockSpec(memory_space=pltpu.VMEM)
HBM = pl.BlockSpec(memory_space=pltpu.HBM)


def group_sums(values):
    lane = lax.broadcasted_iota(jnp.int32, values.shape, 1)
    for bit in (1, 2, 4):
        partner = jnp.where(
            jnp.bitwise_and(lane, bit) == 0,
            pltpu.roll(values, LANES - bit, 1),
            pltpu.roll(values, bit, 1),
        )
        values = values + partner
    return values


def channel_group_sums(sums):
    sums = jnp.sum(sums, axis=0, keepdims=True)
    halves = [sums[:, at : at + LANES] for at in range(0, sums.shape[1], LANES)]
    return jnp.concatenate(
        [group_sums(jnp.broadcast_to(part, (8, LANES)))[0:1] for part in halves], axis=1
    )


def folded(values):
    return values.astype(jnp.float32).reshape(-1, 8, values.shape[-1])


def put_stats(out_ref, total, squares, centre, count):
    mean = channel_group_sums(total) / count
    away = mean - centre
    spread = channel_group_sums(squares) - count * (away * away)
    kind = jnp.bitwise_and(lax.broadcasted_iota(jnp.int32, (1, LANES), 1), 7)
    row = jnp.zeros((1, LANES), jnp.float32)
    for index, part in enumerate(
        (mean[:, :LANES], spread[:, :LANES], mean[:, LANES:], spread[:, LANES:])
    ):
        row = jnp.where(kind == index, part, row)
    out_ref[...] = jnp.broadcast_to(row, out_ref.shape)


def norm_terms(stats_ref, gain_ref, offset_ref, count):
    stats = stats_ref[...]
    devices = stats.shape[0]
    average = jnp.sum(stats, axis=0, keepdims=True) / devices
    away = stats - average
    between = jnp.sum(away * away, axis=0, keepdims=True) / devices
    within = average / count
    kind = jnp.bitwise_and(lax.broadcasted_iota(jnp.int32, (8, LANES), 1), 7)
    row = lax.broadcasted_iota(jnp.int32, (8, LANES), 0)
    terms = jnp.zeros((8, LANES), jnp.float32)
    for index, (lane, part) in enumerate(
        ((0, average), (2, average), (0, between), (2, between))
    ):
        terms = jnp.where(jnp.logical_and(row == index, kind == lane), part, terms)
    for index, lane in ((2, 1), (3, 3)):
        terms = jnp.where(jnp.logical_and(row == index, kind == lane), within, terms)
    terms = group_sums(terms)
    mean = jnp.concatenate([terms[0:1], terms[1:2]], axis=1)
    var = jnp.concatenate([terms[2:3], terms[3:4]], axis=1)
    return mean, (0.5 * gain_ref[...]) / jnp.sqrt(var + EPS), 0.5 * offset_ref[...]


def near_and_far(rows):
    odd = lax.rem(lax.axis_index("rows"), 2)
    return (1 - odd) * (rows - 1), odd * (rows - 1)


def row_place():
    place = lax.axis_index("rows")
    return lax.rem(place, 2) == 1, place > 0, place < lax.axis_size("rows") - 1


def has_past():
    return lax.axis_index("frames") > 0


def active(value, terms, valid):
    mean, scale, offset = terms
    value = (value.astype(jnp.float32) - mean) * scale + offset
    value = value + value * jnp.tanh(value)
    return value if valid is None else jnp.where(valid, value, 0.0)


class Window:
    def __init__(self, wide_ref, terms, cols):
        self.wide_ref, self.terms = wide_ref, terms
        self.cols, self.chans = cols, wide_ref.shape[3]
        self.pairs = wide_ref.shape[2] // cols
        self.rows = 2 * self.pairs
        self.odd, self.above, self.below = row_place()

    def active(self, value, valid):
        return active(value, self.terms, valid)

    def put(self, frame, body, near, far, valid):
        above, below = self.above, self.below
        if valid is not None:
            above, below = jnp.logical_and(above, valid), jnp.logical_and(below, valid)
        lines = [self.active(jnp.where(self.odd, near, far), above)]
        lines += [self.active(body[row], valid) for row in range(self.rows)]
        lines += [self.active(jnp.where(self.odd, far, near), below)]
        for pair in range(self.pairs):
            first, second, third, fourth = lines[2 * pair : 2 * pair + 4]
            mixed = (
                first - third, 0.5 * (second + third), 0.5 * (third - second), second - fourth
            )
            for index, value in enumerate(mixed):
                self.wide_ref[frame, index, pair * self.cols : (pair + 1) * self.cols] = (
                    value.astype(jnp.bfloat16)
                )

    def conv(self, start, count, kernel_ref, mixed_ref, mix=False):
        totals = [None, None]
        for lag_col in LAG_COLS:
            if mix:
                mix_taps(kernel_ref, mixed_ref, lag_col)
            terms = []
            for index in range(4):
                if index in (0, 3):
                    taps = [kernel_ref[lag, 2 * (index // 3), lag_col] for lag in range(3)]
                else:
                    taps = [mixed_ref[index - 1, lag, lag_col] for lag in range(3)]
                terms.append(product(self.wide_ref, start, count, index, taps))
            middle = terms[1] - terms[2]
            parts = terms[0] + (terms[1] + terms[2]), middle - terms[3]
            for at, part in enumerate(parts):
                part = shifted(part, self.cols, lag_col)
                totals[at] = part if totals[at] is None else totals[at] + part
        return [
            [totals[row % 2][frame * self.pairs + row // 2] for row in range(self.rows)]
            for frame in range(count)
        ]


def product(wide_ref, start, count, index, taps):
    window = jnp.concatenate(
        [
            wide_ref[start + lag : start + lag + count, index].reshape(-1, wide_ref.shape[3])
            for lag in range(3)
        ],
        axis=1,
    )
    return jnp.dot(window, jnp.concatenate(taps, axis=0), preferred_element_type=jnp.float32)


def shifted(part, cols, lag_col):
    part = part.reshape(-1, cols, part.shape[-1])
    column = lax.broadcasted_iota(jnp.int32, (1, 8, 1), 1)
    if lag_col == 0:
        part = pltpu.roll(part, 1, 1)
        first = jnp.where(column == 0, 0.0, part[:, :8])
        part = jnp.concatenate([first, part[:, 8:]], axis=1)
    if lag_col == 2:
        part = pltpu.roll(part, cols - 1, 1)
        last = jnp.where(column == 7, 0.0, part[:, cols - 8 :])
        part = jnp.concatenate([part[:, : cols - 8], last], axis=1)
    return part


def mix_taps(kernel_ref, mixed_ref, lag_col):
    for lag in range(3):
        first, second, third = (
            kernel_ref[lag, row, lag_col].astype(jnp.float32) for row in range(3)
        )
        outer = first + third
        mixed_ref[0, lag, lag_col] = (outer + second).astype(jnp.bfloat16)
        mixed_ref[1, lag, lag_col] = (outer - second).astype(jnp.bfloat16)


def past_kernel(values_ref, past_ref):
    past_ref[...] = values_ref[values_ref.shape[0] - LAGS :]


def edges_kernel(values_ref, past_ref, near_ref, far_ref):
    near, far = near_and_far(values_ref.shape[1])
    for row, out_ref in ((near, near_ref), (far, far_ref)):
        out_ref[0:LAGS] = past_ref[:, row]
        out_ref[LAGS:] = values_ref[:, row]


def stats_kernel(values_ref, out_ref):
    frames, rows, cols, chans = values_ref.shape
    count = float(frames * rows * cols * (chans // GROUPS))
    zero = jnp.zeros((8, chans), jnp.float32)

    total = zero
    for index in range(frames):
        total = total + jnp.sum(folded(values_ref[index]), axis=0)
    centre = channel_group_sums(total) / count

    squares = zero
    for index in range(frames):
        away = folded(values_ref[index]) - centre
        squares = squares + jnp.sum(away * away, axis=0)
    put_stats(out_ref, total, squares, centre, count)


def group_count(frames, rows, cols, chans):
    return float(frames * rows * cols * (chans // GROUPS))


def inner_kernel(
    own_ref, past_ref, stats_ref, gain_ref, offset_ref, kernel_ref,
    hidden_ref, partial_ref, middle_ref, sums_ref, wide_ref, side_ref, mixed_ref,
):
    frames, rows, cols, chans = own_ref.shape
    terms = norm_terms(stats_ref, gain_ref, offset_ref, group_count(*own_ref.shape))
    total = jnp.zeros((8, chans), jnp.float32)
    for frame in range(frames + LAGS):
        body, valid = own_ref.at[frame - LAGS], None
        if frame < LAGS:
            body, valid = past_ref.at[frame], has_past()
        lines = [active(body[row], terms, valid) for row in range(rows)]
        for pair in range(2):
            first, second = lines[2 * pair : 2 * pair + 2]
            for index, value in enumerate((0.5 * (first + second), 0.5 * (second - first))):
                wide_ref[frame, index, pair * cols : (pair + 1) * cols] = value.astype(jnp.bfloat16)
            side_ref[frame, pair] = (lines[pair] - lines[pair + 2]).astype(jnp.bfloat16)
            middle_ref[frame, pair] = lines[pair + 1].astype(jnp.bfloat16)
        if frame < STEP + 1 or (frame - 1) % STEP:
            continue
        start = frame - 1 - STEP
        sums = [None, None]
        sides = [None, None]
        for lag_col in LAG_COLS:
            if start == 0:
                mix_taps(kernel_ref, mixed_ref, lag_col)
            taps = [[mixed_ref[at, lag, lag_col] for lag in range(3)] for at in range(2)]
            plus, minus = (product(wide_ref, start, STEP, at, taps[at]) for at in range(2))
            for at, part in enumerate((plus + minus, plus - minus)):
                part = shifted(part, cols, lag_col)
                sums[at] = part if sums[at] is None else sums[at] + part
            for at in range(2):
                taps = [kernel_ref[lag, 2 - 2 * at, lag_col] for lag in range(3)]
                part = shifted(product(side_ref, start, STEP, at, taps), cols, lag_col)
                sides[at] = part if sides[at] is None else sides[at] + part
        for at in range(STEP):
            place = start + at
            partial_ref[place, 0] = sums[0][2 * at]
            partial_ref[place, 1] = sums[1][2 * at + 1]
            for row, value in enumerate(
                (sums[1][2 * at] - sides[0][at], sums[0][2 * at + 1] + sides[1][at])
            ):
                hidden = value.astype(jnp.bfloat16)
                hidden_ref[place, row] = hidden
                if place >= 2:
                    total = total + jnp.sum(folded(hidden), axis=0)
    sums_ref[...] = total


def outer_kernel(
    near_ref, far_ref, stats_ref, gain_ref, offset_ref, kernel_ref,
    hidden_ref, partial_ref, middle_ref, sums_ref,
    out_stats_ref, out_near_ref, out_far_ref, side_ref,
):
    count_frames, rows, cols, chans = hidden_ref.shape
    frames = count_frames - 2
    count = group_count(frames, 2 * rows, cols, chans)
    terms = norm_terms(stats_ref, gain_ref, offset_ref, count)
    odd, above, below = row_place()
    sums = sums_ref[...]
    centre = channel_group_sums(sums) / (count / 2)
    squares = jnp.zeros((8, chans), jnp.float32)

    def square(block):
        away = folded(block) - centre
        return jnp.sum(away * away, axis=0)

    for frame in range(frames + LAGS):
        valids = above, below
        if frame < LAGS:
            valids = [jnp.logical_and(valid, has_past()) for valid in valids]
        near, far = near_ref[frame], far_ref[frame]
        upper = active(jnp.where(odd, near, far), terms, valids[0])
        lower = active(jnp.where(odd, far, near), terms, valids[1])
        middle = [middle_ref[frame, row].astype(jnp.float32) for row in range(2)]
        side_ref[frame, 0] = (upper - middle[0]).astype(jnp.bfloat16)
        side_ref[frame, 1] = (middle[1] - lower).astype(jnp.bfloat16)
        if 2 <= frame < count_frames:
            squares = squares + square(hidden_ref[frame])
        if frame < STEP + 1 or (frame - 1) % STEP:
            continue
        start = frame - 1 - STEP
        sides = [None, None]
        for lag_col in LAG_COLS:
            for at in range(2):
                taps = [kernel_ref[lag, 2 * at, lag_col] for lag in range(3)]
                part = shifted(product(side_ref, start, STEP, at, taps), cols, lag_col)
                sides[at] = part if sides[at] is None else sides[at] + part
        for at in range(STEP):
            place = start + at
            edges = [
                (partial_ref[place, 0] + sides[0][at]).astype(jnp.bfloat16),
                (partial_ref[place, 1] - sides[1][at]).astype(jnp.bfloat16),
            ]
            out_near_ref[place] = jnp.where(odd, edges[0], edges[1])
            out_far_ref[place] = jnp.where(odd, edges[1], edges[0])
            if place >= 2:
                for edge in edges:
                    squares = squares + square(edge)
                    sums = sums + jnp.sum(folded(edge), axis=0)
    put_stats(out_stats_ref, sums, squares, centre, count)


def columns_apart(line, pair_ref):
    cols, chans = line.shape
    halves = range(chans // LANES)
    for half in halves:
        pair_ref[half] = line[:, half * LANES : (half + 1) * LANES]
    return (
        jnp.concatenate([pair_ref[half, pl.ds(k, cols // 2, stride=2)] for half in halves], axis=1)
        for k in range(2)
    )


def second_kernel(
    hidden_ref, own_near_ref, own_far_ref, near_ref, far_ref, stats_ref, gain_ref, offset_ref,
    kernel_ref, source_ref, bias_ref, *rest,
):
    *low_refs, high_ref, wide_ref, mixed_ref, pair_ref, low_ref = rest
    frames, rows, cols, chans = source_ref.shape
    terms = norm_terms(stats_ref, gain_ref, offset_ref, group_count(*source_ref.shape))
    window = Window(wide_ref, terms, cols)
    factor = 0.5**1.5
    bands = len(low_refs)
    width = cols // 2 // bands
    for frame in range(frames + 2):
        near, far = own_near_ref[frame], own_far_ref[frame]
        body = (
            jnp.where(window.odd, near, far), hidden_ref[frame, 0], hidden_ref[frame, 1],
            jnp.where(window.odd, far, near),
        )
        window.put(frame, body, near_ref[frame], far_ref[frame], has_past() if frame < 2 else None)
        if frame < 3 or frame % 2 == 0:
            continue
        start = frame - 3
        index = start // 2
        conv = window.conv(start, 2, kernel_ref, mixed_ref, mix=start == 0)
        summed = [
            [
                source_ref[start + at, row].astype(jnp.float32) + conv[at][row] + bias_ref[...]
                for row in range(rows)
            ]
            for at in range(2)
        ]
        for time_band in range(2):
            mixed = [
                before - after if time_band else before + after
                for before, after in zip(*summed, strict=True)
            ]
            for pair in range(rows // 2):
                upper, lower = mixed[2 * pair], mixed[2 * pair + 1]
                for row_band in range(2):
                    line = (upper - lower if row_band else upper + lower) * factor
                    slot = ((index * 2 + time_band) * (rows // 2) + pair) * 2 + row_band
                    even, uneven = columns_apart(line, pair_ref.at[slot % pair_ref.shape[0]])
                    for col_band in range(2):
                        value = even - uneven if col_band else even + uneven
                        value = value.astype(jnp.bfloat16)
                        band = 4 * time_band + 2 * row_band + col_band
                        if band:
                            high_ref[band - 1, index, pair] = value
                        else:
                            for target in range(bands):
                                low_ref[target, index, pair] = value[
                                    target * width : (target + 1) * width
                                ]
    place = lax.axis_index("rows")
    for index, out_ref in enumerate(low_refs):
        out_ref[...] = low_ref[lax.bitwise_xor(place, index)]

def high_kernel(held_ref, out_ref, sems):
    bands = held_ref.shape[0]
    copies = [
        pltpu.make_async_copy(held_ref.at[at], out_ref.at[at], sems.at[at]) for at in range(bands)
    ]
    for copy in copies:
        copy.start()
    for copy in copies:
        copy.wait()


def low_kernel(*refs):
    *pieces, out_ref, sems = refs
    place = lax.axis_index("rows")
    rows = pieces[0].shape[1]
    copies = [
        pltpu.make_async_copy(
            piece, out_ref.at[:, pl.ds(lax.bitwise_xor(place, index) * rows, rows)], sems.at[index]
        )
        for index, piece in enumerate(pieces)
    ]
    for copy in copies:
        copy.start()
    for copy in copies:
        copy.wait()


def route(shift, pairs):
    frame_count, row_count = lax.axis_size("frames"), lax.axis_size("rows")
    return [
        (f * row_count + r, (f + shift) * row_count + s)
        for f in range(frame_count - shift)
        for r, s in pairs
    ]


def send(values, where):
    return lax.ppermute(values, ("frames", "rows"), where)


def share(stats):
    return lax.all_to_all(stats, ("frames", "rows"), 0, 0, tiled=True)


def half(*shape):
    return jax.ShapeDtypeStruct(shape, jnp.bfloat16)


def single(*shape):
    return jax.ShapeDtypeStruct(shape, jnp.float32)


def call(kernel, name, mib, ins, out_shape, scratch=(), cost=0, spaces=None, out_spaces=None):
    estimate = pl.CostEstimate(flops=cost, bytes_accessed=10**6, transcendentals=0)
    return pl.pallas_call(
        kernel,
        out_shape=out_shape,
        in_specs=spaces or [VMEM] * len(ins),
        out_specs=out_spaces or jax.tree.map(lambda _: VMEM, out_shape),
        scratch_shapes=list(scratch),
        compiler_params=pltpu.CompilerParams(vmem_limit_bytes=mib * 2**20),
        name=name,
        cost_estimate=estimate if cost else None,
    )(*ins)


def body(inputs, kernel_one, gain_one, offset_one, kernel_two, gain_two, offset_two, bias_two):
    frames, rows, cols, chans = inputs.shape
    bands = lax.axis_size("rows")
    devices = lax.axis_size("frames") * bands
    work = 2 * rows * cols * chans * 18 * chans
    to_near = route(0, [(r, r ^ 1) for r in range(bands)])
    to_far = route(0, [(r, ((r + 1) ^ 1) - 1) for r in range(1, bands - 1)])
    to_next = route(1, [(r, r) for r in range(bands)])

    def window(*shape):
        return pltpu.VMEM(shape, jnp.bfloat16)

    past = call(past_kernel, "past", 8, (inputs,), half(LAGS, rows, cols, chans))
    past = send(past, to_next)
    stats = call(stats_kernel, "stats_one", 8, (inputs,), single(devices, LANES), cost=10**10)
    past, stats = lax.optimization_barrier((past, share(stats)))
    reach = frames + LAGS
    near, far = call(
        edges_kernel, "edges", 8, (inputs, past),
        (half(reach, cols, chans), half(reach, cols, chans)),
    )
    near, far = send(near, to_near), send(far, to_far)
    affine = (gain_one[None], offset_one[None])
    inner, partial, middle, sums = call(
        inner_kernel, "conv_inner", 32, (inputs, past, stats, *affine, kernel_one),
        (
            half(frames + 2, 2, cols, chans), single(frames + 2, 2, cols, chans),
            half(reach, 2, cols, chans), single(8, chans),
        ),
        [
            window(reach, 2, 2 * cols, chans), window(reach, 2, cols, chans),
            window(2, 3, 3, chans, chans),
        ],
        cost=work * (frames + 2),
    )
    edge = half(frames + 2, cols, chans)
    stats, own_near, own_far = call(
        outer_kernel, "conv_outer", 32,
        (near, far, stats, *affine, kernel_one, inner, partial, middle, sums),
        (single(devices, LANES), edge, edge), [window(reach, 2, cols, chans)], cost=work * 4,
    )
    near, far = send(own_near, to_near), send(own_far, to_far)
    stats = share(stats)
    piece = half(frames // 2, rows // 2, cols // 2 // bands, chans)
    high = half(7, frames // 2, rows // 2, cols // 2, chans)
    *pieces, high = call(
        second_kernel, "conv_two", 32,
        (
            inner, own_near, own_far, near, far, stats, gain_two[None], offset_two[None], kernel_two, inputs,
            bias_two[None],
        ),
        (*[piece] * bands, high),
        [
            window(frames + 2, 4, rows // 2 * cols, chans), window(2, 3, 3, chans, chans),
            pltpu.VMEM((8, chans // LANES, cols, LANES), jnp.float32),
            window(bands, *piece.shape),
        ],
        cost=work * frames,
    )
    pieces = pieces[:1] + [
        send(pieces[k], route(0, [(r, r ^ k) for r in range(bands)])) for k in range(1, bands)
    ]
    high = call(
        high_kernel, "high_bands", 8, (high,), half(*high.shape),
        [pltpu.SemaphoreType.DMA((high.shape[0],))], cost=10**9, out_spaces=HBM,
    )
    low = call(
        low_kernel, "low_rows", 8, pieces,
        half(frames // 2, bands * (rows // 2), cols // 2 // bands, chans),
        [pltpu.SemaphoreType.DMA((bands,))], out_spaces=HBM,
    )
    return low, high


def solution(mesh):
    in_specs = (P("frames", "rows", None, None), P(), P(), P(), P(), P(), P(), P())
    out_specs = (P("frames", None, "rows", None), P(None, "frames", "rows", None, None))
    return jax.shard_map(body, mesh=mesh, in_specs=in_specs, out_specs=out_specs, check_vma=False)
```

```python
import functools

import jax
import jax.numpy as jnp
from jax import lax
from jax.experimental import pallas as pl
from jax.experimental.pallas import tpu as pltpu
from jax.sharding import PartitionSpec as P

GROUPS = 32
EPS = 1e-06
LANES = 128
LAGS = 4
STEP = 2
LAG_COLS = (1, 0, 2)
VMEM = pl.BlockSpec(memory_space=pltpu.VMEM)
HBM = pl.BlockSpec(memory_space=pltpu.HBM)


def group_sums(values):
    lane = lax.broadcasted_iota(jnp.int32, values.shape, 1)
    for bit in (1, 2, 4):
        partner = jnp.where(
            jnp.bitwise_and(lane, bit) == 0,
            pltpu.roll(values, LANES - bit, 1),
            pltpu.roll(values, bit, 1),
        )
        values = values + partner
    return values


def channel_group_sums(sums):
    sums = jnp.sum(sums, axis=0, keepdims=True)
    halves = [sums[:, at : at + LANES] for at in range(0, sums.shape[1], LANES)]
    return jnp.concatenate(
        [group_sums(jnp.broadcast_to(part, (8, LANES)))[0:1] for part in halves], axis=1
    )


def folded(values):
    return values.astype(jnp.float32).reshape(-1, 8, values.shape[-1])


def put_stats(out_ref, total, squares, centre, count):
    mean = channel_group_sums(total) / count
    away = mean - centre
    spread = channel_group_sums(squares) - count * (away * away)
    kind = jnp.bitwise_and(lax.broadcasted_iota(jnp.int32, (1, LANES), 1), 7)
    row = jnp.zeros((1, LANES), jnp.float32)
    for index, part in enumerate(
        (mean[:, :LANES], spread[:, :LANES], mean[:, LANES:], spread[:, LANES:])
    ):
        row = jnp.where(kind == index, part, row)
    out_ref[...] = jnp.broadcast_to(row, out_ref.shape)


def norm_terms(stats_ref, gain_ref, offset_ref, count):
    stats = stats_ref[...]
    devices = stats.shape[0]
    average = jnp.sum(stats, axis=0, keepdims=True) / devices
    away = stats - average
    between = jnp.sum(away * away, axis=0, keepdims=True) / devices
    within = average / count
    kind = jnp.bitwise_and(lax.broadcasted_iota(jnp.int32, (8, LANES), 1), 7)
    row = lax.broadcasted_iota(jnp.int32, (8, LANES), 0)
    terms = jnp.zeros((8, LANES), jnp.float32)
    for index, (lane, part) in enumerate(
        ((0, average), (2, average), (0, between), (2, between))
    ):
        terms = jnp.where(jnp.logical_and(row == index, kind == lane), part, terms)
    for index, lane in ((2, 1), (3, 3)):
        terms = jnp.where(jnp.logical_and(row == index, kind == lane), within, terms)
    terms = group_sums(terms)
    mean = jnp.concatenate([terms[0:1], terms[1:2]], axis=1)
    var = jnp.concatenate([terms[2:3], terms[3:4]], axis=1)
    return mean, (0.5 * gain_ref[...]) / jnp.sqrt(var + EPS), 0.5 * offset_ref[...]


def near_and_far(rows):
    odd = lax.rem(lax.axis_index("rows"), 2)
    return (1 - odd) * (rows - 1), odd * (rows - 1)


def row_place():
    place = lax.axis_index("rows")
    return lax.rem(place, 2) == 1, place > 0, place < lax.axis_size("rows") - 1


def has_past():
    return lax.axis_index("frames") > 0


def active(value, terms, valid):
    mean, scale, offset = terms
    value = (value.astype(jnp.float32) - mean) * scale + offset
    value = value + value * jnp.tanh(value)
    return value if valid is None else jnp.where(valid, value, 0.0)


class Window:
    def __init__(self, wide_ref, terms, cols):
        self.wide_ref, self.terms = wide_ref, terms
        self.cols, self.chans = cols, wide_ref.shape[3]
        self.pairs = wide_ref.shape[2] // cols
        self.rows = 2 * self.pairs
        self.odd, self.above, self.below = row_place()

    def active(self, value, valid):
        return active(value, self.terms, valid)

    def put(self, frame, body, near, far, valid):
        above, below = self.above, self.below
        if valid is not None:
            above, below = jnp.logical_and(above, valid), jnp.logical_and(below, valid)
        lines = [self.active(jnp.where(self.odd, near, far), above)]
        lines += [self.active(body[row], valid) for row in range(self.rows)]
        lines += [self.active(jnp.where(self.odd, far, near), below)]
        for pair in range(self.pairs):
            first, second, third, fourth = lines[2 * pair : 2 * pair + 4]
            mixed = (
                first - third, 0.5 * (second + third), 0.5 * (third - second), second - fourth
            )
            for index, value in enumerate(mixed):
                self.wide_ref[frame, index, pair * self.cols : (pair + 1) * self.cols] = (
                    value.astype(jnp.bfloat16)
                )

    def conv(self, start, count, kernel_ref, mixed_ref, mix=False):
        totals = [None, None]
        for lag_col in LAG_COLS:
            if mix:
                mix_taps(kernel_ref, mixed_ref, lag_col)
            terms = []
            for index in range(4):
                if index in (0, 3):
                    taps = [kernel_ref[lag, 2 * (index // 3), lag_col] for lag in range(3)]
                else:
                    taps = [mixed_ref[index - 1, lag, lag_col] for lag in range(3)]
                terms.append(product(self.wide_ref, start, count, index, taps))
            middle = terms[1] - terms[2]
            parts = terms[0] + (terms[1] + terms[2]), middle - terms[3]
            for at, part in enumerate(parts):
                part = shifted(part, self.cols, lag_col)
                totals[at] = part if totals[at] is None else totals[at] + part
        return [
            [totals[row % 2][frame * self.pairs + row // 2] for row in range(self.rows)]
            for frame in range(count)
        ]


def product(wide_ref, start, count, index, taps):
    window = jnp.concatenate(
        [
            wide_ref[start + lag : start + lag + count, index].reshape(-1, wide_ref.shape[3])
            for lag in range(3)
        ],
        axis=1,
    )
    return jnp.dot(window, jnp.concatenate(taps, axis=0), preferred_element_type=jnp.float32)


def shifted(part, cols, lag_col):
    part = part.reshape(-1, cols, part.shape[-1])
    column = lax.broadcasted_iota(jnp.int32, (1, 8, 1), 1)
    if lag_col == 0:
        part = pltpu.roll(part, 1, 1)
        first = jnp.where(column == 0, 0.0, part[:, :8])
        part = jnp.concatenate([first, part[:, 8:]], axis=1)
    if lag_col == 2:
        part = pltpu.roll(part, cols - 1, 1)
        last = jnp.where(column == 7, 0.0, part[:, cols - 8 :])
        part = jnp.concatenate([part[:, : cols - 8], last], axis=1)
    return part


def mix_taps(kernel_ref, mixed_ref, lag_col):
    for lag in range(3):
        first, second, third = (
            kernel_ref[lag, row, lag_col].astype(jnp.float32) for row in range(3)
        )
        outer = first + third
        mixed_ref[0, lag, lag_col] = (outer + second).astype(jnp.bfloat16)
        mixed_ref[1, lag, lag_col] = (outer - second).astype(jnp.bfloat16)


def past_kernel(values_ref, past_ref):
    past_ref[...] = values_ref[values_ref.shape[0] - LAGS :]


def edges_kernel(values_ref, past_ref, near_ref, far_ref):
    near, far = near_and_far(values_ref.shape[1])
    for row, out_ref in ((near, near_ref), (far, far_ref)):
        out_ref[0:LAGS] = past_ref[:, row]
        out_ref[LAGS:] = values_ref[:, row]


def stats_kernel(values_ref, out_ref):
    frames, rows, cols, chans = values_ref.shape
    count = float(frames * rows * cols * (chans // GROUPS))
    zero = jnp.zeros((8, chans), jnp.float32)

    total = zero
    for index in range(frames):
        total = total + jnp.sum(folded(values_ref[index]), axis=0)
    centre = channel_group_sums(total) / count

    squares = zero
    for index in range(frames):
        away = folded(values_ref[index]) - centre
        squares = squares + jnp.sum(away * away, axis=0)
    put_stats(out_ref, total, squares, centre, count)


def group_count(frames, rows, cols, chans):
    return float(frames * rows * cols * (chans // GROUPS))


def inner_kernel(
    own_ref, past_ref, stats_ref, gain_ref, offset_ref, kernel_ref,
    hidden_ref, partial_ref, middle_ref, sums_ref, wide_ref, side_ref, mixed_ref,
):
    frames, rows, cols, chans = own_ref.shape
    terms = norm_terms(stats_ref, gain_ref, offset_ref, group_count(*own_ref.shape))
    total = jnp.zeros((8, chans), jnp.float32)
    for frame in range(frames + LAGS):
        body, valid = own_ref.at[frame - LAGS], None
        if frame < LAGS:
            body, valid = past_ref.at[frame], has_past()
        lines = [active(body[row], terms, valid) for row in range(rows)]
        for pair in range(2):
            first, second = lines[2 * pair : 2 * pair + 2]
            for index, value in enumerate((0.5 * (first + second), 0.5 * (second - first))):
                wide_ref[frame, index, pair * cols : (pair + 1) * cols] = value.astype(jnp.bfloat16)
            side_ref[frame, pair] = (lines[pair] - lines[pair + 2]).astype(jnp.bfloat16)
            middle_ref[frame, pair] = lines[pair + 1].astype(jnp.bfloat16)
        if frame < STEP + 1 or (frame - 1) % STEP:
            continue
        start = frame - 1 - STEP
        sums = [None, None]
        sides = [None, None]
        for lag_col in LAG_COLS:
            if start == 0:
                mix_taps(kernel_ref, mixed_ref, lag_col)
            taps = [[mixed_ref[at, lag, lag_col] for lag in range(3)] for at in range(2)]
            plus, minus = (product(wide_ref, start, STEP, at, taps[at]) for at in range(2))
            for at, part in enumerate((plus + minus, plus - minus)):
                part = shifted(part, cols, lag_col)
                sums[at] = part if sums[at] is None else sums[at] + part
            for at in range(2):
                taps = [kernel_ref[lag, 2 - 2 * at, lag_col] for lag in range(3)]
                part = shifted(product(side_ref, start, STEP, at, taps), cols, lag_col)
                sides[at] = part if sides[at] is None else sides[at] + part
        for at in range(STEP):
            place = start + at
            partial_ref[place, 0] = sums[0][2 * at]
            partial_ref[place, 1] = sums[1][2 * at + 1]
            for row, value in enumerate(
                (sums[1][2 * at] - sides[0][at], sums[0][2 * at + 1] + sides[1][at])
            ):
                hidden = value.astype(jnp.bfloat16)
                hidden_ref[place, row] = hidden
                if place >= 2:
                    total = total + jnp.sum(folded(hidden), axis=0)
    sums_ref[...] = total


def outer_kernel(
    near_ref, far_ref, stats_ref, gain_ref, offset_ref, kernel_ref,
    hidden_ref, partial_ref, middle_ref, sums_ref,
    out_stats_ref, out_near_ref, out_far_ref, side_ref,
):
    count_frames, rows, cols, chans = hidden_ref.shape
    frames = count_frames - 2
    count = group_count(frames, 2 * rows, cols, chans)
    terms = norm_terms(stats_ref, gain_ref, offset_ref, count)
    odd, above, below = row_place()
    sums = sums_ref[...]
    centre = channel_group_sums(sums) / (count / 2)
    squares = jnp.zeros((8, chans), jnp.float32)

    def square(block):
        away = folded(block) - centre
        return jnp.sum(away * away, axis=0)

    for frame in range(frames + LAGS):
        valids = above, below
        if frame < LAGS:
            valids = [jnp.logical_and(valid, has_past()) for valid in valids]
        near, far = near_ref[frame], far_ref[frame]
        upper = active(jnp.where(odd, near, far), terms, valids[0])
        lower = active(jnp.where(odd, far, near), terms, valids[1])
        middle = [middle_ref[frame, row].astype(jnp.float32) for row in range(2)]
        side_ref[frame, 0] = (upper - middle[0]).astype(jnp.bfloat16)
        side_ref[frame, 1] = (middle[1] - lower).astype(jnp.bfloat16)
        if 2 <= frame < count_frames:
            squares = squares + square(hidden_ref[frame])
        if frame < STEP + 1 or (frame - 1) % STEP:
            continue
        start = frame - 1 - STEP
        sides = [None, None]
        for lag_col in LAG_COLS:
            for at in range(2):
                taps = [kernel_ref[lag, 2 * at, lag_col] for lag in range(3)]
                part = shifted(product(side_ref, start, STEP, at, taps), cols, lag_col)
                sides[at] = part if sides[at] is None else sides[at] + part
        for at in range(STEP):
            place = start + at
            edges = [
                (partial_ref[place, 0] + sides[0][at]).astype(jnp.bfloat16),
                (partial_ref[place, 1] - sides[1][at]).astype(jnp.bfloat16),
            ]
            out_near_ref[place] = jnp.where(odd, edges[0], edges[1])
            out_far_ref[place] = jnp.where(odd, edges[1], edges[0])
            if place >= 2:
                for edge in edges:
                    squares = squares + square(edge)
                    sums = sums + jnp.sum(folded(edge), axis=0)
    put_stats(out_stats_ref, sums, squares, centre, count)


def columns_apart(line, pair_ref):
    cols, chans = line.shape
    halves = range(chans // LANES)
    for half in halves:
        pair_ref[half] = line[:, half * LANES : (half + 1) * LANES]
    return (
        jnp.concatenate([pair_ref[half, pl.ds(k, cols // 2, stride=2)] for half in halves], axis=1)
        for k in range(2)
    )


def second_kernel(
    hidden_ref, own_near_ref, own_far_ref, near_ref, far_ref, stats_ref, gain_ref, offset_ref,
    kernel_ref, source_ref, bias_ref, *rest,
):
    *low_refs, high_ref, wide_ref, mixed_ref, pair_ref, low_ref = rest
    frames, rows, cols, chans = source_ref.shape
    terms = norm_terms(stats_ref, gain_ref, offset_ref, group_count(*source_ref.shape))
    window = Window(wide_ref, terms, cols)
    factor = 0.5**1.5
    bands = len(low_refs)
    width = cols // 2 // bands
    for frame in range(frames + 2):
        near, far = own_near_ref[frame], own_far_ref[frame]
        body = (
            jnp.where(window.odd, near, far), hidden_ref[frame, 0], hidden_ref[frame, 1],
            jnp.where(window.odd, far, near),
        )
        window.put(frame, body, near_ref[frame], far_ref[frame], has_past() if frame < 2 else None)
        if frame < 3 or frame % 2 == 0:
            continue
        start = frame - 3
        index = start // 2
        conv = window.conv(start, 2, kernel_ref, mixed_ref, mix=start == 0)
        summed = [
            [
                source_ref[start + at, row].astype(jnp.float32) + conv[at][row] + bias_ref[...]
                for row in range(rows)
            ]
            for at in range(2)
        ]
        for time_band in range(2):
            mixed = [
                before - after if time_band else before + after
                for before, after in zip(*summed, strict=True)
            ]
            for pair in range(rows // 2):
                upper, lower = mixed[2 * pair], mixed[2 * pair + 1]
                for row_band in range(2):
                    line = (upper - lower if row_band else upper + lower) * factor
                    slot = ((index * 2 + time_band) * (rows // 2) + pair) * 2 + row_band
                    even, uneven = columns_apart(line, pair_ref.at[slot % pair_ref.shape[0]])
                    for col_band in range(2):
                        value = even - uneven if col_band else even + uneven
                        value = value.astype(jnp.bfloat16)
                        band = 4 * time_band + 2 * row_band + col_band
                        if band:
                            high_ref[band - 1, index, pair] = value
                        else:
                            for target in range(bands):
                                low_ref[target, index, pair] = value[
                                    target * width : (target + 1) * width
                                ]
    place = lax.axis_index("rows")
    for index, out_ref in enumerate(low_refs):
        out_ref[...] = low_ref[lax.bitwise_xor(place, index)]

def high_kernel(held_ref, out_ref, sems):
    bands = held_ref.shape[0]
    copies = [
        pltpu.make_async_copy(held_ref.at[at], out_ref.at[at], sems.at[at]) for at in range(bands)
    ]
    for copy in copies:
        copy.start()
    for copy in copies:
        copy.wait()


def low_kernel(*refs):
    *pieces, out_ref, sems = refs
    place = lax.axis_index("rows")
    rows = pieces[0].shape[1]
    copies = [
        pltpu.make_async_copy(
            piece, out_ref.at[:, pl.ds(lax.bitwise_xor(place, index) * rows, rows)], sems.at[index]
        )
        for index, piece in enumerate(pieces)
    ]
    for copy in copies:
        copy.start()
    for copy in copies:
        copy.wait()


def route(shift, pairs):
    frame_count, row_count = lax.axis_size("frames"), lax.axis_size("rows")
    return [
        (f * row_count + r, (f + shift) * row_count + s)
        for f in range(frame_count - shift)
        for r, s in pairs
    ]


def send(values, where):
    return lax.ppermute(values, ("frames", "rows"), where)


def share(stats):
    return lax.all_to_all(stats, ("frames", "rows"), 0, 0, tiled=True)


def half(*shape):
    return jax.ShapeDtypeStruct(shape, jnp.bfloat16)


def single(*shape):
    return jax.ShapeDtypeStruct(shape, jnp.float32)


def call(kernel, name, mib, ins, out_shape, scratch=(), cost=0, spaces=None, out_spaces=None):
    estimate = pl.CostEstimate(flops=cost, bytes_accessed=10**6, transcendentals=0)
    return pl.pallas_call(
        kernel,
        out_shape=out_shape,
        in_specs=spaces or [VMEM] * len(ins),
        out_specs=out_spaces or jax.tree.map(lambda _: VMEM, out_shape),
        scratch_shapes=list(scratch),
        compiler_params=pltpu.CompilerParams(vmem_limit_bytes=mib * 2**20),
        name=name,
        cost_estimate=estimate if cost else None,
    )(*ins)


def body(inputs, kernel_one, gain_one, offset_one, kernel_two, gain_two, offset_two, bias_two):
    frames, rows, cols, chans = inputs.shape
    bands = lax.axis_size("rows")
    devices = lax.axis_size("frames") * bands
    work = 2 * rows * cols * chans * 18 * chans
    to_near = route(0, [(r, r ^ 1) for r in range(bands)])
    to_far = route(0, [(r, ((r + 1) ^ 1) - 1) for r in range(1, bands - 1)])
    to_far += [
        (f * bands + r, (f ^ 8) * bands + r)
        for f in range(lax.axis_size("frames"))
        for r in (0, bands - 1)
    ]
    to_next = route(1, [(r, r) for r in range(bands)])
    to_next += [((devices - bands) + r, r) for r in range(bands)]

    def window(*shape):
        return pltpu.VMEM(shape, jnp.bfloat16)

    past = call(past_kernel, "past", 8, (inputs,), half(LAGS, rows, cols, chans))
    past = send(past, to_next)
    stats = call(stats_kernel, "stats_one", 8, (inputs,), single(devices, LANES), cost=10**10)
    past, stats = lax.optimization_barrier((past, share(stats)))
    reach = frames + LAGS
    near, far = call(
        edges_kernel, "edges", 8, (inputs, past),
        (half(reach, cols, chans), half(reach, cols, chans)),
    )
    near, far = send(near, to_near), send(far, to_far)
    affine = (gain_one[None], offset_one[None])
    inner, partial, middle, sums = call(
        inner_kernel, "conv_inner", 32, (inputs, past, stats, *affine, kernel_one),
        (
            half(frames + 2, 2, cols, chans), single(frames + 2, 2, cols, chans),
            half(reach, 2, cols, chans), single(8, chans),
        ),
        [
            window(reach, 2, 2 * cols, chans), window(reach, 2, cols, chans),
            window(2, 3, 3, chans, chans),
        ],
        cost=work * (frames + 2),
    )
    edge = half(frames + 2, cols, chans)
    stats, own_near, own_far = call(
        outer_kernel, "conv_outer", 32,
        (near, far, stats, *affine, kernel_one, inner, partial, middle, sums),
        (single(devices, LANES), edge, edge), [window(reach, 2, cols, chans)], cost=work * 4,
    )
    near, far = send(own_near, to_near), send(own_far, to_far)
    stats = share(stats)
    piece = half(frames // 2, rows // 2, cols // 2 // bands, chans)
    high = half(7, frames // 2, rows // 2, cols // 2, chans)
    *pieces, high = call(
        second_kernel, "conv_two", 32,
        (
            inner, own_near, own_far, near, far, stats, gain_two[None], offset_two[None], kernel_two, inputs,
            bias_two[None],
        ),
        (*[piece] * bands, high),
        [
            window(frames + 2, 4, rows // 2 * cols, chans), window(2, 3, 3, chans, chans),
            pltpu.VMEM((8, chans // LANES, cols, LANES), jnp.float32),
            window(bands, *piece.shape),
        ],
        cost=work * frames,
    )
    pieces = pieces[:1] + [
        send(pieces[k], route(0, [(r, r ^ k) for r in range(bands)])) for k in range(1, bands)
    ]
    high = call(
        high_kernel, "high_bands", 8, (high,), half(*high.shape),
        [pltpu.SemaphoreType.DMA((high.shape[0],))], cost=10**9, out_spaces=HBM,
    )
    low = call(
        low_kernel, "low_rows", 8, pieces,
        half(frames // 2, bands * (rows // 2), cols // 2 // bands, chans),
        [pltpu.SemaphoreType.DMA((bands,))], out_spaces=HBM,
    )
    return low, high


def solution(mesh):
    in_specs = (P("frames", "rows", None, None), P(), P(), P(), P(), P(), P(), P())
    out_specs = (P("frames", None, "rows", None), P(None, "frames", "rows", None, None))
    return jax.shard_map(body, mesh=mesh, in_specs=in_specs, out_specs=out_specs, check_vma=False)
```

```python
import functools

import jax
import jax.numpy as jnp
from jax import lax
from jax.experimental import pallas as pl
from jax.experimental.pallas import tpu as pltpu
from jax.sharding import PartitionSpec as P

GROUPS = 32
EPS = 1e-06
LANES = 128
LAGS = 4
OUTER_STEP = 2
INNER_STEPS, SECOND_STEPS = (4, 2, 4), (2, 2, 2, 2)
LAG_COLS = (1, 0, 2)
VMEM = pl.BlockSpec(memory_space=pltpu.VMEM)
HBM = pl.BlockSpec(memory_space=pltpu.HBM)


def group_sums(values):
    lane = lax.broadcasted_iota(jnp.int32, values.shape, 1)
    for bit in (1, 2, 4):
        partner = jnp.where(
            jnp.bitwise_and(lane, bit) == 0,
            pltpu.roll(values, LANES - bit, 1),
            pltpu.roll(values, bit, 1),
        )
        values = values + partner
    return values


def channel_group_sums(sums):
    sums = jnp.sum(sums, axis=0, keepdims=True)
    halves = [sums[:, at : at + LANES] for at in range(0, sums.shape[1], LANES)]
    return jnp.concatenate(
        [group_sums(jnp.broadcast_to(part, (8, LANES)))[0:1] for part in halves], axis=1
    )


def folded(values):
    return values.astype(jnp.float32).reshape(-1, 8, values.shape[-1])


def put_stats(out_ref, mean, away, squares, count):
    spread = channel_group_sums(squares) - count * (away * away)
    kind = jnp.bitwise_and(lax.broadcasted_iota(jnp.int32, (1, LANES), 1), 7)
    row = jnp.zeros((1, LANES), jnp.float32)
    for index, part in enumerate(
        (mean[:, :LANES], spread[:, :LANES], mean[:, LANES:], spread[:, LANES:])
    ):
        row = jnp.where(kind == index, part, row)
    out_ref[...] = jnp.broadcast_to(row, out_ref.shape)


def norm_terms(stats_ref, gain_ref, offset_ref, count):
    stats = stats_ref[...]
    devices = stats.shape[0]
    average = jnp.sum(stats, axis=0, keepdims=True) / devices
    away = stats - average
    between = jnp.sum(away * away, axis=0, keepdims=True) / devices
    within = average / count
    kind = jnp.bitwise_and(lax.broadcasted_iota(jnp.int32, (8, LANES), 1), 7)
    row = lax.broadcasted_iota(jnp.int32, (8, LANES), 0)
    terms = jnp.zeros((8, LANES), jnp.float32)
    for index, (lane, part) in enumerate(
        ((0, average), (2, average), (0, between), (2, between))
    ):
        terms = jnp.where(jnp.logical_and(row == index, kind == lane), part, terms)
    for index, lane in ((2, 1), (3, 3)):
        terms = jnp.where(jnp.logical_and(row == index, kind == lane), within, terms)
    terms = group_sums(terms)
    mean = jnp.concatenate([terms[0:1], terms[1:2]], axis=1)
    var = jnp.concatenate([terms[2:3], terms[3:4]], axis=1)
    return mean, (0.5 * gain_ref[...]) / jnp.sqrt(var + EPS), 0.5 * offset_ref[...]


def near_and_far(rows):
    odd = lax.rem(lax.axis_index("rows"), 2)
    return (1 - odd) * (rows - 1), odd * (rows - 1)


def row_place():
    place = lax.axis_index("rows")
    return lax.rem(place, 2) == 1, place > 0, place < lax.axis_size("rows") - 1


def has_past():
    return lax.axis_index("frames") > 0


def active(value, terms, valid):
    mean, scale, offset = terms
    value = (value.astype(jnp.float32) - mean) * scale + offset
    value = value + value * jnp.tanh(value)
    return value if valid is None else jnp.where(valid, value, 0.0)


class Window:
    def __init__(self, wide_ref, terms, cols):
        self.wide_ref, self.terms = wide_ref, terms
        self.cols, self.chans = cols, wide_ref.shape[3]
        self.pairs = wide_ref.shape[2] // cols
        self.rows = 2 * self.pairs
        self.odd, self.above, self.below = row_place()

    def active(self, value, valid):
        return active(value, self.terms, valid)

    def put(self, frame, body, near, far, valid):
        above, below = self.above, self.below
        if valid is not None:
            above, below = jnp.logical_and(above, valid), jnp.logical_and(below, valid)
        lines = [self.active(jnp.where(self.odd, near, far), above)]
        lines += [self.active(body[row], valid) for row in range(self.rows)]
        lines += [self.active(jnp.where(self.odd, far, near), below)]
        for pair in range(self.pairs):
            first, second, third, fourth = lines[2 * pair : 2 * pair + 4]
            mixed = (
                first - third, 0.5 * (second + third), 0.5 * (third - second), second - fourth
            )
            for index, value in enumerate(mixed):
                self.wide_ref[frame, index, pair * self.cols : (pair + 1) * self.cols] = (
                    value.astype(jnp.bfloat16)
                )

    def conv(self, start, count, kernel_ref, mixed_ref, mix=False):
        totals = [None, None]
        for lag_col in LAG_COLS:
            if mix:
                mix_taps(kernel_ref, mixed_ref, lag_col)
            terms = []
            for index in range(4):
                if index in (0, 3):
                    taps = [kernel_ref[lag, 2 * (index // 3), lag_col] for lag in range(3)]
                else:
                    taps = [mixed_ref[index - 1, lag, lag_col] for lag in range(3)]
                terms.append(product(self.wide_ref, start, count, index, taps))
            middle = terms[1] - terms[2]
            parts = terms[0] + (terms[1] + terms[2]), middle - terms[3]
            for at, part in enumerate(parts):
                part = shifted(part, self.cols, lag_col)
                totals[at] = part if totals[at] is None else totals[at] + part
        return [
            [totals[row % 2][frame * self.pairs + row // 2] for row in range(self.rows)]
            for frame in range(count)
        ]


def product(wide_ref, start, count, index, taps):
    window = jnp.concatenate(
        [
            wide_ref[start + lag : start + lag + count, index].reshape(-1, wide_ref.shape[3])
            for lag in range(3)
        ],
        axis=1,
    )
    return jnp.dot(window, jnp.concatenate(taps, axis=0), preferred_element_type=jnp.float32)


def shifted(part, cols, lag_col):
    part = part.reshape(-1, cols, part.shape[-1])
    column = lax.broadcasted_iota(jnp.int32, (1, 8, 1), 1)
    if lag_col == 0:
        part = pltpu.roll(part, 1, 1)
        first = jnp.where(column == 0, 0.0, part[:, :8])
        part = jnp.concatenate([first, part[:, 8:]], axis=1)
    if lag_col == 2:
        part = pltpu.roll(part, cols - 1, 1)
        last = jnp.where(column == 7, 0.0, part[:, cols - 8 :])
        part = jnp.concatenate([part[:, : cols - 8], last], axis=1)
    return part


def mix_taps(kernel_ref, mixed_ref, lag_col):
    for lag in range(3):
        first, second, third = (
            kernel_ref[lag, row, lag_col].astype(jnp.float32) for row in range(3)
        )
        outer = first + third
        mixed_ref[0, lag, lag_col] = (outer + second).astype(jnp.bfloat16)
        mixed_ref[1, lag, lag_col] = (outer - second).astype(jnp.bfloat16)


def past_kernel(values_ref, past_ref):
    past_ref[...] = values_ref[values_ref.shape[0] - LAGS :]


def edges_kernel(values_ref, past_ref, near_ref, far_ref):
    near, far = near_and_far(values_ref.shape[1])
    for row, out_ref in ((near, near_ref), (far, far_ref)):
        out_ref[0:LAGS] = past_ref[:, row]
        out_ref[LAGS:] = values_ref[:, row]


def stats_kernel(values_ref, out_ref):
    frames, rows, cols, chans = values_ref.shape
    count = float(frames * rows * cols * (chans // GROUPS))
    total = squares = jnp.zeros((8, chans), jnp.float32)
    sample = jnp.sum(folded(values_ref[0, 0]), axis=0)
    centre = channel_group_sums(sample) / (cols * (chans // GROUPS))
    for index in range(frames):
        away = folded(values_ref[index]) - centre
        total = total + jnp.sum(away, axis=0)
        squares = squares + jnp.sum(away * away, axis=0)
    away = channel_group_sums(total) / count
    put_stats(out_ref, centre + away, away, squares, count)


def group_count(frames, rows, cols, chans):
    return float(frames * rows * cols * (chans // GROUPS))


def inner_kernel(
    own_ref, past_ref, stats_ref, gain_ref, offset_ref, kernel_ref,
    hidden_ref, partial_ref, middle_ref, sums_ref, wide_ref, side_ref, mixed_ref,
):
    frames, rows, cols, chans = own_ref.shape
    terms = norm_terms(stats_ref, gain_ref, offset_ref, group_count(*own_ref.shape))
    total = jnp.zeros((8, chans), jnp.float32)
    start, steps = 0, list(INNER_STEPS)
    for frame in range(frames + LAGS):
        body, valid = own_ref.at[frame - LAGS], None
        if frame < LAGS:
            body, valid = past_ref.at[frame], has_past()
        lines = [active(body[row], terms, valid) for row in range(rows)]
        for pair in range(2):
            first, second = lines[2 * pair : 2 * pair + 2]
            for index, value in enumerate((0.5 * (first + second), 0.5 * (second - first))):
                wide_ref[frame, index, pair * cols : (pair + 1) * cols] = value.astype(jnp.bfloat16)
            side_ref[frame, pair] = (lines[pair] - lines[pair + 2]).astype(jnp.bfloat16)
            middle_ref[frame, pair] = lines[pair + 1].astype(jnp.bfloat16)
        if not steps or frame < start + steps[0] + 1:
            continue
        count = steps.pop(0)
        sums = [None, None]
        sides = [None, None]
        for lag_col in LAG_COLS:
            if start == 0:
                mix_taps(kernel_ref, mixed_ref, lag_col)
            taps = [[mixed_ref[at, lag, lag_col] for lag in range(3)] for at in range(2)]
            plus, minus = (product(wide_ref, start, count, at, taps[at]) for at in range(2))
            for at, part in enumerate((plus + minus, plus - minus)):
                part = shifted(part, cols, lag_col)
                sums[at] = part if sums[at] is None else sums[at] + part
            for at in range(2):
                taps = [kernel_ref[lag, 2 - 2 * at, lag_col] for lag in range(3)]
                part = shifted(product(side_ref, start, count, at, taps), cols, lag_col)
                sides[at] = part if sides[at] is None else sides[at] + part
        for at in range(count):
            place = start + at
            partial_ref[place, 0] = sums[0][2 * at]
            partial_ref[place, 1] = sums[1][2 * at + 1]
            for row, value in enumerate(
                (sums[1][2 * at] - sides[0][at], sums[0][2 * at + 1] + sides[1][at])
            ):
                hidden = value.astype(jnp.bfloat16)
                hidden_ref[place, row] = hidden
                if place >= 2:
                    total = total + jnp.sum(folded(hidden), axis=0)
        start += count
    sums_ref[...] = total


def outer_kernel(
    near_ref, far_ref, stats_ref, gain_ref, offset_ref, kernel_ref,
    hidden_ref, partial_ref, middle_ref, sums_ref,
    out_stats_ref, out_near_ref, out_far_ref, side_ref,
):
    count_frames, rows, cols, chans = hidden_ref.shape
    frames = count_frames - 2
    count = group_count(frames, 2 * rows, cols, chans)
    terms = norm_terms(stats_ref, gain_ref, offset_ref, count)
    odd, above, below = row_place()
    sums = sums_ref[...]
    centre = channel_group_sums(sums) / (count / 2)
    squares = jnp.zeros((8, chans), jnp.float32)

    def square(block):
        away = folded(block) - centre
        return jnp.sum(away * away, axis=0)

    for frame in range(frames + LAGS):
        valids = above, below
        if frame < LAGS:
            valids = [jnp.logical_and(valid, has_past()) for valid in valids]
        near, far = near_ref[frame], far_ref[frame]
        upper = active(jnp.where(odd, near, far), terms, valids[0])
        lower = active(jnp.where(odd, far, near), terms, valids[1])
        middle = [middle_ref[frame, row].astype(jnp.float32) for row in range(2)]
        side_ref[frame, 0] = (upper - middle[0]).astype(jnp.bfloat16)
        side_ref[frame, 1] = (middle[1] - lower).astype(jnp.bfloat16)
        if 2 <= frame < count_frames:
            squares = squares + square(hidden_ref[frame])
        if frame < OUTER_STEP + 1 or (frame - 1) % OUTER_STEP:
            continue
        start = frame - 1 - OUTER_STEP
        sides = [None, None]
        for lag_col in LAG_COLS:
            for at in range(2):
                taps = [kernel_ref[lag, 2 * at, lag_col] for lag in range(3)]
                part = shifted(product(side_ref, start, OUTER_STEP, at, taps), cols, lag_col)
                sides[at] = part if sides[at] is None else sides[at] + part
        for at in range(OUTER_STEP):
            place = start + at
            edges = [
                (partial_ref[place, 0] + sides[0][at]).astype(jnp.bfloat16),
                (partial_ref[place, 1] - sides[1][at]).astype(jnp.bfloat16),
            ]
            out_near_ref[place] = jnp.where(odd, edges[0], edges[1])
            out_far_ref[place] = jnp.where(odd, edges[1], edges[0])
            if place >= 2:
                for edge in edges:
                    squares = squares + square(edge)
                    sums = sums + jnp.sum(folded(edge), axis=0)
    mean = channel_group_sums(sums) / count
    put_stats(out_stats_ref, mean, mean - centre, squares, count)


def columns_apart(line, pair_ref):
    cols, chans = line.shape
    halves = range(chans // LANES)
    for half in halves:
        pair_ref[half] = line[:, half * LANES : (half + 1) * LANES]
    return (
        jnp.concatenate([pair_ref[half, pl.ds(k, cols // 2, stride=2)] for half in halves], axis=1)
        for k in range(2)
    )


def second_kernel(
    hidden_ref, own_near_ref, own_far_ref, near_ref, far_ref, stats_ref, gain_ref, offset_ref,
    kernel_ref, source_ref, bias_ref, *rest,
):
    *low_refs, high_ref, wide_ref, mixed_ref, pair_ref, low_ref = rest
    frames, rows, cols, chans = source_ref.shape
    terms = norm_terms(stats_ref, gain_ref, offset_ref, group_count(*source_ref.shape))
    window = Window(wide_ref, terms, cols)
    factor = 0.5**1.5
    bands = len(low_refs)
    width = cols // 2 // bands
    done, steps = [], list(SECOND_STEPS)
    for frame in range(frames + 2):
        near, far = own_near_ref[frame], own_far_ref[frame]
        body = (
            jnp.where(window.odd, near, far), hidden_ref[frame, 0], hidden_ref[frame, 1],
            jnp.where(window.odd, far, near),
        )
        window.put(frame, body, near_ref[frame], far_ref[frame], has_past() if frame < 2 else None)
        start = len(done)
        if not steps or frame < start + steps[0] + 1:
            continue
        done += window.conv(start, steps.pop(0), kernel_ref, mixed_ref, mix=start == 0)
        for index in range(start // 2, len(done) // 2):
            summed = [
                [
                    source_ref[own, row].astype(jnp.float32) + done[own][row] + bias_ref[...]
                    for row in range(rows)
                ]
                for own in (2 * index, 2 * index + 1)
            ]
            for time_band in range(2):
                mixed = [
                    before - after if time_band else before + after
                    for before, after in zip(*summed, strict=True)
                ]
                for pair in range(rows // 2):
                    upper, lower = mixed[2 * pair], mixed[2 * pair + 1]
                    for row_band in range(2):
                        line = (upper - lower if row_band else upper + lower) * factor
                        slot = ((index * 2 + time_band) * (rows // 2) + pair) * 2 + row_band
                        even, uneven = columns_apart(line, pair_ref.at[slot % pair_ref.shape[0]])
                        for col_band in range(2):
                            value = even - uneven if col_band else even + uneven
                            value = value.astype(jnp.bfloat16)
                            band = 4 * time_band + 2 * row_band + col_band
                            if band:
                                high_ref[band - 1, index, pair] = value
                            else:
                                for target in range(bands):
                                    low_ref[target, index, pair] = value[
                                        target * width : (target + 1) * width
                                    ]
    place = lax.axis_index("rows")
    for index, out_ref in enumerate(low_refs):
        out_ref[...] = low_ref[lax.bitwise_xor(place, index)]

def high_kernel(held_ref, out_ref, sems):
    bands = held_ref.shape[0]
    copies = [
        pltpu.make_async_copy(held_ref.at[at], out_ref.at[at], sems.at[at]) for at in range(bands)
    ]
    for copy in copies:
        copy.start()
    for copy in copies:
        copy.wait()


def low_kernel(*refs):
    *pieces, out_ref, sems = refs
    place = lax.axis_index("rows")
    rows = pieces[0].shape[1]
    copies = [
        pltpu.make_async_copy(
            piece, out_ref.at[:, pl.ds(lax.bitwise_xor(place, index) * rows, rows)], sems.at[index]
        )
        for index, piece in enumerate(pieces)
    ]
    for copy in copies:
        copy.start()
    for copy in copies:
        copy.wait()


def route(shift, pairs):
    frame_count, row_count = lax.axis_size("frames"), lax.axis_size("rows")
    return [
        (f * row_count + r, (f + shift) * row_count + s)
        for f in range(frame_count - shift)
        for r, s in pairs
    ]


def send(values, where):
    return lax.ppermute(values, ("frames", "rows"), where)


def share(stats):
    return lax.all_to_all(stats, ("frames", "rows"), 0, 0, tiled=True)


def half(*shape):
    return jax.ShapeDtypeStruct(shape, jnp.bfloat16)


def single(*shape):
    return jax.ShapeDtypeStruct(shape, jnp.float32)


def call(kernel, name, mib, ins, out_shape, scratch=(), cost=0, spaces=None, out_spaces=None):
    estimate = pl.CostEstimate(flops=cost, bytes_accessed=10**6, transcendentals=0)
    return pl.pallas_call(
        kernel,
        out_shape=out_shape,
        in_specs=spaces or [VMEM] * len(ins),
        out_specs=out_spaces or jax.tree.map(lambda _: VMEM, out_shape),
        scratch_shapes=list(scratch),
        compiler_params=pltpu.CompilerParams(vmem_limit_bytes=mib * 2**20),
        name=name,
        cost_estimate=estimate if cost else None,
    )(*ins)


def body(inputs, kernel_one, gain_one, offset_one, kernel_two, gain_two, offset_two, bias_two):
    frames, rows, cols, chans = inputs.shape
    bands = lax.axis_size("rows")
    devices = lax.axis_size("frames") * bands
    work = 2 * rows * cols * chans * 18 * chans
    to_near = route(0, [(r, r ^ 1) for r in range(bands)])
    to_far = route(0, [(r, ((r + 1) ^ 1) - 1) for r in range(1, bands - 1)])
    to_far += [
        (f * bands + r, (f ^ 8) * bands + r)
        for f in range(lax.axis_size("frames"))
        for r in (0, bands - 1)
    ]
    to_next = route(1, [(r, r) for r in range(bands)])
    to_next += [((devices - bands) + r, r) for r in range(bands)]

    def window(*shape):
        return pltpu.VMEM(shape, jnp.bfloat16)

    past = call(past_kernel, "past", 8, (inputs,), half(LAGS, rows, cols, chans))
    past = send(past, to_next)
    stats = call(stats_kernel, "stats_one", 8, (inputs,), single(devices, LANES), cost=10**10)
    past, stats = lax.optimization_barrier((past, share(stats)))
    reach = frames + LAGS
    near, far = call(
        edges_kernel, "edges", 8, (inputs, past),
        (half(reach, cols, chans), half(reach, cols, chans)),
    )
    near, far = send(near, to_near), send(far, to_far)
    affine = (gain_one[None], offset_one[None])
    inner, partial, middle, sums = call(
        inner_kernel, "conv_inner", 32, (inputs, past, stats, *affine, kernel_one),
        (
            half(frames + 2, 2, cols, chans), single(frames + 2, 2, cols, chans),
            half(reach, 2, cols, chans), single(8, chans),
        ),
        [
            window(reach, 2, 2 * cols, chans), window(reach, 2, cols, chans),
            window(2, 3, 3, chans, chans),
        ],
        cost=work * (frames + 2),
    )
    edge = half(frames + 2, cols, chans)
    stats, own_near, own_far = call(
        outer_kernel, "conv_outer", 32,
        (near, far, stats, *affine, kernel_one, inner, partial, middle, sums),
        (single(devices, LANES), edge, edge), [window(reach, 2, cols, chans)], cost=work * 4,
    )
    near, far = send(own_near, to_near), send(own_far, to_far)
    stats = share(stats)
    piece = half(frames // 2, rows // 2, cols // 2 // bands, chans)
    high = half(7, frames // 2, rows // 2, cols // 2, chans)
    *pieces, high = call(
        second_kernel, "conv_two", 32,
        (
            inner, own_near, own_far, near, far, stats, gain_two[None], offset_two[None], kernel_two, inputs,
            bias_two[None],
        ),
        (*[piece] * bands, high),
        [
            window(frames + 2, 4, rows // 2 * cols, chans), window(2, 3, 3, chans, chans),
            pltpu.VMEM((8, chans // LANES, cols, LANES), jnp.float32),
            window(bands, *piece.shape),
        ],
        cost=work * frames,
    )
    pieces = pieces[:1] + [
        send(pieces[k], route(0, [(r, r ^ k) for r in range(bands)])) for k in range(1, bands)
    ]
    high = call(
        high_kernel, "high_bands", 8, (high,), half(*high.shape),
        [pltpu.SemaphoreType.DMA((high.shape[0],))], cost=10**9, out_spaces=HBM,
    )
    low = call(
        low_kernel, "low_rows", 8, pieces,
        half(frames // 2, bands * (rows // 2), cols // 2 // bands, chans),
        [pltpu.SemaphoreType.DMA((bands,))], out_spaces=HBM,
    )
    return low, high


def solution(mesh):
    in_specs = (P("frames", "rows", None, None), P(), P(), P(), P(), P(), P(), P())
    out_specs = (P("frames", None, "rows", None), P(None, "frames", "rows", None, None))
    return jax.shard_map(body, mesh=mesh, in_specs=in_specs, out_specs=out_specs, check_vma=False)
```
